32 devices in a mesh: section: 4 (over y, x), zone: 8 (over z, core).
Axes of the slice: x: 2, y: 2, z: 4, core: 2. Of those that a mesh axis runs over, the one named last changes fastest.
Arguments:
- tiles: bfloat16 [4, 256, 128, 128], P('section', 'zone'), may hold values from -0.5 to 0.5
- tile_row: int32 [4, 256], P('section', 'zone'), may hold values from 0 to 19
- tile_col: int32 [4, 256], P('section', 'zone'), may hold values from 0 to 15, as said below
- tile_live: int32 [4, 256], P('section', 'zone'), may hold values from 0 to 1, as said below
- block_place: int32 [16], replicated, may hold values from 0 to 15, as said below
- demand: int32 [4, 20480, 128], P('section', 'zone'), may hold values from 0 to 15
- flow_cost: float32 [4, 2048], P('section', 'zone'), may hold values from -6 to 6
- stock_cost: float32 [4, 20480], P('section', 'zone'), may hold values from 0.1 to 1
- flows: float32 [4, 2048, 128], P('section', 'zone'), may hold values from 0 to 1
- stock: float32 [4, 20480, 128], P('section', 'zone'), may hold values from 0 to 2
- duals: float32 [4, 20480, 128], P('section', 'zone'), may hold values from -6 to 6
Outputs:
- flows_out: float32 [4, 2048, 128], P('section', 'zone')
- stock_out: float32 [4, 20480, 128], P('section', 'zone')
- duals_out: float32 [4, 20480, 128], P('section', 'zone')
The draws below stay inside these ranges and needn't reach their ends.
Inputs may be any that keep to these rules, and one draw needn't show every extreme that they name: `tile_col`: flow block ids. For each phase and zone band, at most 4 live slots name flow blocks whose position // 2 is one given band; in each phase one band receives exactly 4 such slots from every zone band. `tile_live`: live flags of the slots, with the counts described for tile_col. `block_place`: A permutation of the flow blocks.
All inputs are finite; a program needn't handle non-finite values.
Results may differ from the reference program's by a relative error of at most 0.019.
Values may be sent and summed in bfloat16 or wider, within the bound.
No kernel may reach another device: no remote copies, remote signals or barrier semaphores. Data moves between devices by JAX's collectives and lax.ppermute only.
A program may use at most 128 MiB of HBM per device.

```python
import math
import jax
import jax.numpy as jnp
from jax import lax

TILE = 128
ZT_DEV = 20
SC = 128
CAP = 4
FB_DEV = 2
ITERS = 2
PHASES = 4
ZONES = 20480
BLOCKS = 16
FLOWS = 2048
SLOTS = 32
TILE_LIST = 256
N_ZONE = 8


def slot_layout(key):
    placing = jax.random.permutation(jax.random.fold_in(key, 11), BLOCKS).astype(jnp.int32)
    inverse = jnp.argsort(placing).astype(jnp.int32)
    counts = jax.random.randint(jax.random.fold_in(key, 12), (PHASES, N_ZONE, N_ZONE), 1, CAP + 1)
    filled = jax.random.randint(jax.random.fold_in(key, 13), (PHASES,), 0, N_ZONE)
    owners = jnp.arange(N_ZONE, dtype=jnp.int32)
    counts = jnp.where(owners[None, None, :] == filled[:, None, None], CAP, counts)
    slot_ids = jnp.arange(SLOTS, dtype=jnp.int32)
    slot_owner = slot_ids // CAP
    live_flag = ((slot_ids % CAP)[None, None, :] < jnp.repeat(counts, CAP, axis=2)).astype(jnp.int32)
    offsets = jax.random.randint(jax.random.fold_in(key, 14), (PHASES, N_ZONE, SLOTS), 0, FB_DEV)
    stored = slot_owner[None, None, :] * FB_DEV + offsets
    logical = inverse[stored]
    scores = jax.random.randint(jax.random.fold_in(key, 15), (PHASES, N_ZONE, SLOTS), 0, 1048576) * SLOTS + slot_ids[None, None, :]
    order = jnp.argsort(scores, axis=-1)
    live_flag = jnp.take_along_axis(live_flag, order, axis=-1)
    logical = jnp.take_along_axis(logical, order, axis=-1)
    return (placing, logical.reshape(PHASES, N_ZONE * SLOTS).astype(jnp.int32), live_flag.reshape(PHASES, N_ZONE * SLOTS).astype(jnp.int32))


def draw_block_place(key, part):
    return slot_layout(key)[0]


def draw_tile_col(key, part):
    return slot_layout(key)[1]


def draw_tile_live(key, part):
    return slot_layout(key)[2]


def touch_ends(entries, stream_key, low, largest):
    spot = [jax.random.randint(jax.random.fold_in(stream_key, axis), (), 0, length) for axis, length in enumerate(entries.shape)]
    longest = entries.shape.index(max(entries.shape))
    next_to = spot[:longest] + [(spot[longest] + 1) % entries.shape[longest]] + spot[longest + 1:]
    return entries.at[tuple(spot)].set(low).at[tuple(next_to)].set(largest)


def block_levels(own_key, extent, shards, low, largest):
    level = 1.0
    for dim, blocks in shards:
        draws = jax.random.uniform(jax.random.fold_in(jax.random.fold_in(own_key, 6), dim), (blocks,), jnp.float32, low / len(shards), largest / len(shards))
        level = level * jnp.repeat(jnp.exp(draws), extent[dim] // blocks).reshape((-1,) + (1,) * (len(extent) - 1 - dim))
    return level


def normal_values(key, shape, deviation, reach, shards=(), kind=jnp.bfloat16):
    level = block_levels(key, shape, shards, -0.22, 0.18) if shards else 1.0
    array = jax.random.normal(key, shape, jnp.float32) * deviation * level
    return jnp.minimum(jnp.maximum(array, -reach), reach).astype(kind)


def setup_inputs(seed: int = 0) -> dict:
    arg_keys = jax.random.split(jax.random.key(seed), 12)
    tiles = normal_values(arg_keys[0], (PHASES, TILE_LIST, TILE, TILE), TILE ** -0.5, 0.5, ((0, 4), (1, 8)))
    tile_row = touch_ends(jax.random.randint(arg_keys[1], (PHASES, TILE_LIST), 0, ZT_DEV), jax.random.fold_in(arg_keys[1], 1), 0, ZT_DEV - 1).astype(jnp.int32)
    tile_col = draw_tile_col(jax.random.fold_in(arg_keys[11], 71), 0)
    tile_live = draw_tile_live(jax.random.fold_in(arg_keys[11], 71), 0)
    block_place = draw_block_place(jax.random.fold_in(arg_keys[11], 71), 0)
    demand = touch_ends(jax.random.randint(arg_keys[5], (PHASES, ZONES, SC), 0, 16), jax.random.fold_in(arg_keys[5], 1), 0, 15).astype(jnp.int32)
    flow_cost = normal_values(arg_keys[6], (PHASES, FLOWS), 1.0, 6.0, ((0, 4), (1, 8)), jnp.float32)
    stock_cost = jnp.clip(jnp.exp(math.log(1.0) - 2.3025851 * jax.random.uniform(arg_keys[7], (PHASES, ZONES), jnp.float32) ** block_levels(arg_keys[7], (PHASES, ZONES), ((0, 4), (1, 8)), -0.2, 0.2)), 0.1, 1.0)
    flows = jnp.clip(1.0 * jax.random.uniform(arg_keys[8], (PHASES, FLOWS, SC), jnp.float32) ** block_levels(arg_keys[8], (PHASES, FLOWS, SC), ((0, 4), (1, 8)), -0.2, 0.2), 0.0, 1.0)
    stock = jnp.clip(2.0 * jax.random.uniform(arg_keys[9], (PHASES, ZONES, SC), jnp.float32) ** block_levels(arg_keys[9], (PHASES, ZONES, SC), ((0, 4), (1, 8)), -0.2, 0.2), 0.0, 2.0)
    duals = normal_values(arg_keys[10], (PHASES, ZONES, SC), 1.0, 6.0, ((0, 4), (1, 8)), jnp.float32)
    return {"tiles": tiles, "tile_row": tile_row, "tile_col": tile_col, "tile_live": tile_live, "block_place": block_place, "demand": demand, "flow_cost": flow_cost, "stock_cost": stock_cost, "flows": flows, "stock": stock, "duals": duals}


STEP_PRIMAL = 0.25
STEP_DUAL = 0.25


def transposed_phase(packed):
    tile_part, global_row, position, alive, dual_phase = packed
    dual_half = dual_phase.astype(jnp.bfloat16).reshape(ZONES // TILE, TILE, SC)
    picked = dual_half[global_row].astype(jnp.float32)
    partial_value = jnp.einsum("kij,kic->kjc", tile_part.astype(jnp.float32), picked).astype(jnp.bfloat16)
    partial_value = lax.optimization_barrier(partial_value).astype(jnp.float32) * alive[:, None, None]
    summed = jax.ops.segment_sum(partial_value, position, num_segments=BLOCKS)
    return summed.reshape(BLOCKS * TILE, SC)


def forward_phase(packed):
    tile_part, global_row, position, alive, flow_half = packed
    blocks_view = flow_half.reshape(BLOCKS, TILE, SC)
    picked = blocks_view[position].astype(jnp.float32)
    products = jnp.einsum("kij,kjc->kic", tile_part.astype(jnp.float32), picked) * alive[:, None, None]
    summed = jax.ops.segment_sum(products, global_row, num_segments=ZONES // TILE)
    return summed.reshape(ZONES, SC)


def reference(tiles, tile_row, tile_col, tile_live, block_place, demand, flow_cost, stock_cost, flows, stock, duals):
    band_index = jnp.arange(TILE_LIST, dtype=jnp.int32) // SLOTS
    global_row = (band_index[None, :] * ZT_DEV + tile_row).astype(jnp.int32)
    position = block_place[tile_col].astype(jnp.int32)
    alive = tile_live.astype(jnp.float32)
    demand_rhs = demand.astype(jnp.float32) * 0.25
    for iteration in range(ITERS):
        pulled = lax.map(transposed_phase, (tiles, global_row, position, alive, duals))
        dual_after = jnp.roll(duals, -1, axis=0)
        new_flows = jnp.maximum(flows - STEP_PRIMAL * (flow_cost[:, :, None] - pulled), 0.0)
        new_stock = jnp.maximum(stock - STEP_PRIMAL * (stock_cost[:, :, None] - dual_after + duals), 0.0)
        flows_bar = 2.0 * new_flows - flows
        stock_bar = 2.0 * new_stock - stock
        pushed = lax.map(forward_phase, (tiles, global_row, position, alive, flows_bar.astype(jnp.bfloat16)))
        stock_before = jnp.roll(stock_bar, 1, axis=0)
        duals = duals + STEP_DUAL * (demand_rhs - (pushed + stock_before - stock_bar))
        flows = new_flows
        stock = new_stock
    return flows, stock, duals
```

```python
import functools

import jax
import jax.numpy as jnp
from jax import lax
from jax.experimental import pallas as pl
from jax.experimental.pallas import tpu as pltpu
from jax.sharding import PartitionSpec as P

ITERS = 2

STEP_PRIMAL = 0.25
STEP_DUAL = 0.25

BF = jnp.bfloat16
F32 = jnp.float32
VMEM = pl.BlockSpec(memory_space=pltpu.VMEM)
SMEM = pl.BlockSpec(memory_space=pltpu.SMEM)
LIMIT = 48 * 1024 * 1024
CORES = 2


def rotate(value, axis, by):
    size = lax.axis_size(axis)
    return lax.ppermute(value, axis, [(i, (i + by) % size) for i in range(size)])


def rotate_chip(value, by):
    size = lax.axis_size("zone")
    return lax.ppermute(value, "zone", [(i, (i + by * CORES) % size) for i in range(size)])


def swap_core(value):
    size = lax.axis_size("zone")
    return lax.ppermute(value, "zone", [(i, i ^ 1) for i in range(size)])


def call(kernel, outs, scratch, flops, moved, *args, smem=0):
    return pl.pallas_call(
        kernel,
        out_shape=outs,
        in_specs=[SMEM] * smem + [VMEM] * (len(args) - smem),
        out_specs=jax.tree.map(lambda _: VMEM, outs),
        scratch_shapes=scratch,
        compiler_params=pltpu.CompilerParams(vmem_limit_bytes=LIMIT),
        cost_estimate=pl.CostEstimate(flops=flops, bytes_accessed=moved, transcendentals=0),
    )(*args)


def quarter_rows(by, parts, size):
    part = lax.rem(lax.axis_index("section") + by, parts)
    return pl.ds(pl.multiple_of(part * size, size), size)


def pack_kernel(parts, size, tile, duals, stock, cost, *packets):
    pieces = size // tile
    for r in range(parts):
        part = lax.rem(lax.axis_index("section") + r, parts)
        rows = pl.ds(pl.multiple_of(part * size, size), size)
        packets[r][0:size] = duals[rows, :].astype(BF)
        packets[r][size : 2 * size] = stock[rows, :].astype(BF)
        tail = packets[r].shape[0] - 2 * size
        lines = [
            cost[:, pl.ds(pl.multiple_of(part * size + i * tile, tile), tile)]
            for i in range(pieces)
        ]
        lines.append(jnp.zeros((tail - pieces, tile), F32))
        packets[r][2 * size : 2 * size + tail] = jnp.concatenate(lines, axis=0).astype(BF)


def block_slot(place, col, live, k, shape, sign):
    chips, owned = shape
    zone = lax.axis_index("zone")
    chip, core = lax.div(zone, CORES), lax.rem(zone, CORES)
    position = place[col[0, k]]
    owner, inner = lax.div(position, owned), lax.rem(position, owned)
    away = lax.rem(sign * (lax.div(owner, CORES) - chip) + chips, chips)
    half = jnp.where(lax.rem(owner, CORES) == core, 0, chips * owned)
    return half + away * owned + inner


def pull_slots(shape, row, col, live, place, tiles, half, acc):
    slots = tiles.shape[0]
    blocks = acc.shape[0] - 1
    acc[...] = jnp.zeros_like(acc)

    def step(k, carry):
        there = jnp.where(live[0, k] == 1, block_slot(place, col, live, k, shape, 1), blocks)
        acc[there] += lax.dot_general(
            tiles[k], half[row[0, k]], (((0,), (0,)), ((), ())), preferred_element_type=F32
        )
        return carry

    lax.fori_loop(0, slots, step, 0, unroll=8)


def push_slots(shape, row, col, live, place, tiles, blocks, acc):
    slots = tiles.shape[0]
    spare = acc.shape[0] - 1

    def step(k, carry):
        there = jnp.where(live[0, k] == 1, row[0, k], spare)
        acc[there] += jnp.dot(
            tiles[k],
            blocks[block_slot(place, col, live, k, shape, -1)],
            preferred_element_type=F32,
        )
        return carry

    lax.fori_loop(0, slots, step, 0, unroll=8)


def give_partials(acc, keep, send):
    n = keep.shape[0]
    keep[...] = acc[0:n].astype(BF)
    send[...] = acc[n : 2 * n].astype(BF)


def pull_kernel(shape, row, col, live, place, tiles, duals, keep, send, half, acc):
    half[...] = duals[...].astype(BF)
    pull_slots(shape, row, col, live, place, tiles, half, acc)
    give_partials(acc, keep, send)


def step_duals(shape, parts, size, refs, blocks, acc):
    row, col, live, place, tiles, duals, demand, near, far = refs[:9]
    combined = refs[9:]
    n = near.shape[0]
    blocks[0:n] = near[...]
    blocks[n : 2 * n] = far[...]
    pieces = size // tiles.shape[1]
    for r in range(parts):
        part = lax.rem(lax.axis_index("section") + r, parts)
        rows = pl.ds(part * pieces, pieces)
        acc[rows] = (
            duals[rows]
            + (STEP_DUAL * 0.25) * demand[rows].astype(F32)
            - STEP_DUAL * combined[r][...].astype(F32)
        )
    push_slots(shape, row, col, live, place, tiles, blocks, acc)


def push_pull_kernel(shape, parts, size, *refs):
    ins, rest = refs[: 9 + parts], refs[9 + parts :]
    next_duals, keep, send = rest[:3]
    packets = rest[3 : 3 + parts]
    blocks, half, acc, acc_blocks = rest[3 + parts :]
    row, col, live, place, tiles = ins[:5]
    step_duals(shape, parts, size, ins, blocks, acc)
    n = next_duals.shape[0]
    next_duals[...] = acc[0:n]
    half[...] = acc[0:n].astype(BF)
    pieces = size // tiles.shape[1]
    for r in range(parts):
        part = lax.rem(lax.axis_index("section") + r, parts)
        packets[r][...] = half[pl.ds(part * pieces, pieces)]
    pull_slots(shape, row, col, live, place, tiles, half, acc_blocks)
    give_partials(acc_blocks, keep, send)


def push_kernel(shape, parts, size, *refs):
    ins = refs[: 9 + parts]
    next_duals, blocks, acc = refs[9 + parts :]
    step_duals(shape, parts, size, ins, blocks, acc)
    next_duals[...] = acc[0 : next_duals.shape[0]]


def spread_cost(line, eye, ones):
    return jnp.dot(jnp.where(eye, line, jnp.zeros_like(line)), ones, preferred_element_type=F32)


def eye_of(tile):
    return lax.broadcasted_iota(jnp.int32, (tile, tile), 0) == lax.broadcasted_iota(
        jnp.int32, (tile, tile), 1
    )


def stock_step(parts, tile, i, costs, dual, stock, eye, ones):
    new = []
    for r in range(parts):
        cost = spread_cost(costs[r][i : i + 1], eye, ones)
        change = cost - dual[(r - 1) % parts] + dual[r]
        new.append(jnp.maximum(stock[r] - STEP_PRIMAL * change, 0.0))
    return new


def first_stock_kernel(parts, size, tile, *refs):
    packets, stocks, combined = refs[:parts], refs[parts], refs[parts + 1 :]
    eye, ones = eye_of(tile), jnp.ones((tile, tile), BF)
    costs = [packets[r][2 * size :].astype(F32).astype(BF) for r in range(parts)]
    for i in range(size // tile):
        rows = slice(i * tile, (i + 1) * tile)
        behind = slice(size + i * tile, size + (i + 1) * tile)
        dual = [packets[r][rows].astype(F32) for r in range(parts)]
        stock = [packets[r][behind].astype(F32) for r in range(parts)]
        new = stock_step(parts, tile, i, costs, dual, stock, eye, ones)
        bar = [2.0 * new[r] - stock[r] for r in range(parts)]
        for r in range(parts):
            stocks[r, rows] = new[r]
            combined[r][rows] = (bar[(r + 1) % parts] - bar[r]).astype(BF)


def last_stock_kernel(parts, size, tile, *refs):
    packets, stocks, duals = refs[:parts], refs[parts], refs[parts + 1 : 2 * parts + 1]
    combined, moved = refs[2 * parts + 1 : 3 * parts + 1], refs[3 * parts + 1 :]
    eye, ones = eye_of(tile), jnp.ones((tile, tile), BF)
    costs = [packets[r][2 * size :].astype(F32).astype(BF) for r in range(parts)]
    for i in range(size // tile):
        rows = slice(i * tile, (i + 1) * tile)
        dual = [duals[r][rows].astype(F32) for r in range(parts)]
        stock = [stocks[r, rows] for r in range(parts)]
        new = stock_step(parts, tile, i, costs, dual, stock, eye, ones)
        bar = [2.0 * new[r] - stock[r] for r in range(parts)]
        for r in range(parts):
            moved[r][rows] = new[r].astype(BF)
            combined[r][rows] = (bar[(r + 1) % parts] - bar[r]).astype(BF)


def place_kernel(parts, size, *refs):
    out = refs[parts]
    for r in range(parts):
        out[quarter_rows(r, parts, size), :] = refs[r][...].astype(F32)


def per_device(
    tiles,
    tile_row,
    tile_col,
    tile_live,
    block_place,
    demand,
    flow_cost,
    stock_cost,
    flows,
    stock,
    duals,
):
    unused_phases, slots, tile, unused_tile = tiles.shape
    scenarios = flows.shape[2]
    rows = duals.shape[1]
    parts = lax.axis_size("section")
    zones = lax.axis_size("zone")
    chips = zones // CORES
    blocks = block_place.shape[0]
    owned = blocks // zones
    band_tiles = rows // tile
    size = rows // parts
    shape = (chips, owned)
    tail = -(-(size // tile) // 16) * 16

    tiles = tiles.reshape(slots, tile, tile)
    duals2 = duals.reshape(rows, scenarios)
    stock2 = stock.reshape(rows, scenarios)
    flows2 = flows.reshape(owned * tile, scenarios)
    duals3 = duals.reshape(band_tiles, tile, scenarios)
    demand3 = demand.reshape(band_tiles, tile, scenarios)
    where = (tile_row, tile_col, tile_live, block_place)
    flops = 2 * slots * tile * tile * scenarios
    quarter = jax.ShapeDtypeStruct((size, scenarios), BF)
    quarter3 = jax.ShapeDtypeStruct((size // tile, tile, scenarios), BF)
    half_blocks = jax.ShapeDtypeStruct((blocks // 2, tile, scenarios), BF)
    pull_scratch = [
        pltpu.VMEM((band_tiles, tile, scenarios), BF),
        pltpu.VMEM((blocks + 1, tile, scenarios), F32),
    ]
    push_scratch = [
        pltpu.VMEM((blocks, tile, scenarios), BF),
        pltpu.VMEM((band_tiles + 1, tile, scenarios), F32),
    ]

    def collect(keep, send):
        both = (keep.astype(F32) + swap_core(send).astype(F32)).astype(BF)
        parts_of = [both[k * owned : (k + 1) * owned] for k in range(chips)]
        got = [rotate_chip(parts_of[k], k) for k in range(1, chips)]
        total = parts_of[0].astype(F32)
        for value in got:
            total = total + value.astype(F32)
        return total.reshape(owned * tile, scenarios)

    def spread(value):
        own = [value] + [rotate_chip(value, k) for k in range(1, chips)]
        near = jnp.concatenate(own, axis=0).reshape(blocks // 2, tile, scenarios)
        return near, swap_core(near)

    def step_flows(now, pulled):
        new = jnp.maximum(now - STEP_PRIMAL * (flow_cost[0][:, None] - pulled), 0.0)
        return new, ((2.0 * new - now).astype(BF) * BF(-STEP_DUAL))

    packets = call(
        functools.partial(pack_kernel, parts, size, tile),
        [jax.ShapeDtypeStruct((2 * size + tail, scenarios), BF)] * parts,
        [],
        0,
        12 * rows * scenarios,
        duals2,
        stock2,
        stock_cost,
    )
    packets = [packets[0]] + [rotate(packets[r], "section", r) for r in range(1, parts)]

    keep, send = call(
        functools.partial(pull_kernel, shape),
        [half_blocks, half_blocks],
        pull_scratch,
        flops,
        4 * rows * scenarios + 2 * slots * tile * tile,
        *where,
        tiles,
        duals3,
        smem=4,
    )
    pulled = collect(keep, send)
    flows1, bar1 = step_flows(flows2, pulled)
    near, far = spread(bar1)

    stocks, *combined = call(
        functools.partial(first_stock_kernel, parts, size, tile),
        [jax.ShapeDtypeStruct((parts, size, scenarios), F32)] + [quarter] * parts,
        [],
        0,
        10 * rows * scenarios,
        *packets,
    )
    combined = [combined[0]] + [rotate(combined[r], "section", -r) for r in range(1, parts)]
    combined = [c.reshape(size // tile, tile, scenarios) for c in combined]

    duals1, keep, send, *halves = call(
        functools.partial(push_pull_kernel, shape, parts, size),
        [jax.ShapeDtypeStruct((band_tiles, tile, scenarios), F32), half_blocks, half_blocks]
        + [quarter3] * parts,
        [push_scratch[0], pull_scratch[0], push_scratch[1], pull_scratch[1]],
        2 * flops,
        16 * rows * scenarios + 2 * slots * tile * tile,
        *where,
        tiles,
        duals3,
        demand3,
        near,
        far,
        *combined,
        smem=4,
    )
    halves = [h.reshape(size, scenarios) for h in halves]
    halves = [halves[0]] + [rotate(halves[r], "section", r) for r in range(1, parts)]
    pulled = collect(keep, send)
    flows2_out, bar2 = step_flows(flows1, pulled)
    near, far = spread(bar2)

    outs = call(
        functools.partial(last_stock_kernel, parts, size, tile),
        [quarter] * (2 * parts),
        [],
        0,
        10 * rows * scenarios,
        *packets,
        stocks,
        *halves,
    )
    combined, moved = outs[:parts], outs[parts:]
    combined = [combined[0]] + [rotate(combined[r], "section", -r) for r in range(1, parts)]
    combined = [c.reshape(size // tile, tile, scenarios) for c in combined]
    moved = [moved[0]] + [rotate(moved[r], "section", -r) for r in range(1, parts)]

    duals_out = call(
        functools.partial(push_kernel, shape, parts, size),
        jax.ShapeDtypeStruct((band_tiles, tile, scenarios), F32),
        push_scratch,
        flops,
        14 * rows * scenarios + 2 * slots * tile * tile,
        *where,
        tiles,
        duals1,
        demand3,
        near,
        far,
        *combined,
        smem=4,
    )
    stock_out = call(
        functools.partial(place_kernel, parts, size),
        jax.ShapeDtypeStruct((rows, scenarios), F32),
        [],
        0,
        6 * rows * scenarios,
        *moved,
    )
    return (
        flows2_out.reshape(flows.shape),
        stock_out.reshape(stock.shape),
        duals_out.reshape(duals.shape),
    )


def solution(mesh):
    in_specs = (
        P("section", "zone", None, None),
        P("section", "zone"),
        P("section", "zone"),
        P("section", "zone"),
        P(),
        P("section", "zone", None),
        P("section", "zone"),
        P("section", "zone"),
        P("section", "zone", None),
        P("section", "zone", None),
        P("section", "zone", None),
    )
    out_specs = (P("section", "zone", None), P("section", "zone", None), P("section", "zone", None))
    return jax.shard_map(
        per_device, mesh=mesh, in_specs=in_specs, out_specs=out_specs, check_vma=False
    )
```

```python
import functools

import jax
import jax.numpy as jnp
from jax import lax
from jax.experimental import pallas as pl
from jax.experimental.pallas import tpu as pltpu
from jax.sharding import PartitionSpec as P

ITERS = 2

STEP_PRIMAL = 0.25
STEP_DUAL = 0.25

BF = jnp.bfloat16
F32 = jnp.float32
VMEM = pl.BlockSpec(memory_space=pltpu.VMEM)
SMEM = pl.BlockSpec(memory_space=pltpu.SMEM)
LIMIT = 48 * 1024 * 1024
FULL = 62 * 1024 * 1024
CORES = 2
STEP_COST = 20_000_000_000


def rotate(value, axis, by):
    size = lax.axis_size(axis)
    return lax.ppermute(value, axis, [(i, (i + by) % size) for i in range(size)])


def rotate_chip(value, by):
    size = lax.axis_size("zone")
    return lax.ppermute(value, "zone", [(i, (i + by * CORES) % size) for i in range(size)])


def swap_core(value):
    size = lax.axis_size("zone")
    return lax.ppermute(value, "zone", [(i, i ^ 1) for i in range(size)])


def after(values, others):
    return lax.optimization_barrier((*values, *others))[: len(values)]


def call(kernel, outs, scratch, flops, moved, *args, smem=0):
    return pl.pallas_call(
        kernel,
        out_shape=outs,
        in_specs=[SMEM] * smem + [VMEM] * (len(args) - smem),
        out_specs=jax.tree.map(lambda _: VMEM, outs),
        scratch_shapes=scratch,
        compiler_params=pltpu.CompilerParams(vmem_limit_bytes=LIMIT),
        cost_estimate=pl.CostEstimate(flops=flops, bytes_accessed=moved, transcendentals=0),
    )(*args)


def quarter_rows(by, parts, size):
    part = lax.rem(lax.axis_index("section") + by, parts)
    return pl.ds(pl.multiple_of(part * size, size), size)


def give_packet(part, size, tile, duals, stock, cost, packet):
    pieces = size // tile
    rows = pl.ds(pl.multiple_of(part * size, size), size)
    packet[0:size] = duals[rows, :].astype(BF)
    packet[size : 2 * size] = stock[rows, :].astype(BF)
    tail = packet.shape[0] - 2 * size
    lines = [
        cost[:, pl.ds(pl.multiple_of(part * size + i * tile, tile), tile)] for i in range(pieces)
    ]
    lines.append(jnp.zeros((tail - pieces, tile), F32))
    packet[2 * size : 2 * size + tail] = jnp.concatenate(lines, axis=0).astype(BF)


def block_slot(place, col, live, k, shape, sign):
    chips, owned = shape
    zone = lax.axis_index("zone")
    chip, core = lax.div(zone, CORES), lax.rem(zone, CORES)
    position = place[col[0, k]]
    owner, inner = lax.div(position, owned), lax.rem(position, owned)
    away = lax.rem(sign * (lax.div(owner, CORES) - chip) + chips, chips)
    half = jnp.where(lax.rem(owner, CORES) == core, 0, chips * owned)
    return half + away * owned + inner


def pull_slots(shape, row, col, live, place, tiles, half, acc):
    slots = tiles.shape[0]
    blocks = acc.shape[0] - 1
    acc[...] = jnp.zeros_like(acc)

    def step(k, carry):
        there = jnp.where(live[0, k] == 1, block_slot(place, col, live, k, shape, 1), blocks)
        acc[there] += lax.dot_general(
            tiles[k], half[row[0, k]], (((0,), (0,)), ((), ())), preferred_element_type=F32
        )
        return carry

    lax.fori_loop(0, slots, step, 0, unroll=8)


def push_slots(shape, row, col, live, place, tiles, blocks, acc):
    slots = tiles.shape[0]
    spare = acc.shape[0] - 1

    def step(k, carry):
        there = jnp.where(live[0, k] == 1, row[0, k], spare)
        acc[there] += jnp.dot(
            tiles[k],
            blocks[block_slot(place, col, live, k, shape, -1)],
            preferred_element_type=F32,
        )
        return carry

    lax.fori_loop(0, slots, step, 0, unroll=8)


def give_partials(acc, keep, send):
    n = keep.shape[0]
    keep[...] = acc[0:n].astype(BF)
    send[...] = acc[n : 2 * n].astype(BF)


def pull_kernel(shape, parts, size, *refs):
    count = 8
    ins, outs = refs[:count], refs[count : count + 2 + parts]
    rest = refs[count + 2 + parts :]
    held, packets, (half, acc, in_sems, out_sems) = rest[:count], rest[count:-4], rest[-4:]
    copies = [pltpu.make_async_copy(ins[i], held[i], in_sems.at[i]) for i in range(count)]
    for i in (5, 6, 7, 0, 1, 2, 3, 4):
        copies[i].start()
    row, col, live, place, tiles, duals, stock, cost = held
    keep, send = outs[:2]
    tile = tiles.shape[1]
    for i in (5, 6, 7):
        copies[i].wait()
    gives = []
    for r in range(parts):
        part = lax.rem(lax.axis_index("section") + r, parts)
        give_packet(part, size, tile, duals, stock, cost, packets[r])
        gives.append(pltpu.make_async_copy(packets[r], outs[2 + r], out_sems.at[r]))
        gives[r].start()
    half[...] = duals[...].astype(BF).reshape(half.shape)
    for i in range(5):
        copies[i].wait()
    pull_slots(shape, row, col, live, place, tiles, half, acc)
    give_partials(acc, keep, send)
    for give in gives:
        give.wait()


def step_duals(shape, parts, size, refs, blocks, acc):
    row, col, live, place, tiles, duals, demand, near, far = refs[:9]
    combined = refs[9:]
    n = near.shape[0]
    blocks[0:n] = near[...]
    blocks[n : 2 * n] = far[...]
    pieces = size // tiles.shape[1]
    for r in range(parts):
        part = lax.rem(lax.axis_index("section") + r, parts)
        rows = pl.ds(part * pieces, pieces)
        acc[rows] = (
            duals[rows]
            + (STEP_DUAL * 0.25) * demand[rows].astype(F32)
            - STEP_DUAL * combined[r][...].astype(F32)
        )
    push_slots(shape, row, col, live, place, tiles, blocks, acc)


def push_pull_kernel(shape, parts, size, *refs):
    ins, rest = refs[: 9 + parts], refs[9 + parts :]
    next_duals, keep, send = rest[:3]
    packets = rest[3 : 3 + parts]
    blocks, half, acc, acc_blocks = rest[3 + parts :]
    row, col, live, place, tiles = ins[:5]
    step_duals(shape, parts, size, ins, blocks, acc)
    n = next_duals.shape[0]
    next_duals[...] = acc[0:n]
    half[...] = acc[0:n].astype(BF)
    pieces = size // tiles.shape[1]
    for r in range(parts):
        part = lax.rem(lax.axis_index("section") + r, parts)
        packets[r][...] = half[pl.ds(part * pieces, pieces)]
    pull_slots(shape, row, col, live, place, tiles, half, acc_blocks)
    give_partials(acc_blocks, keep, send)


def push_kernel(shape, *refs):
    row, col, live, place, tiles, duals, demand, near, far, base, blocks, acc = refs
    n = near.shape[0]
    blocks[0:n] = near[...]
    blocks[n : 2 * n] = far[...]
    n = base.shape[0]
    acc[0:n] = duals[...] + (STEP_DUAL * 0.25) * demand[...].astype(F32)
    push_slots(shape, row, col, live, place, tiles, blocks, acc)
    base[...] = acc[0:n]


def final_kernel(parts, size, *refs):
    base, moved, (duals_out, stock_out) = refs[0], refs[1 : 1 + parts], refs[1 + parts : 3 + parts]
    duals, stock, sems = refs[3 + parts :]
    copies = []
    for r in range(parts):
        part = lax.rem(lax.axis_index("section") + r, parts)
        rows = pl.ds(pl.multiple_of(part * size, size), size)
        duals[rows, :] = base[rows, :] - STEP_DUAL * moved[r][0:size].astype(F32)
        stock[rows, :] = moved[r][size:].astype(F32)
        for i, (held, out) in enumerate(((duals, duals_out), (stock, stock_out))):
            copies.append(pltpu.make_async_copy(held.at[rows], out.at[rows], sems.at[2 * r + i]))
            copies[-1].start()
    for copy in copies:
        copy.wait()


def spread_cost(line, eye, ones):
    return jnp.dot(jnp.where(eye, line, jnp.zeros_like(line)), ones, preferred_element_type=F32)


def eye_of(tile):
    return lax.broadcasted_iota(jnp.int32, (tile, tile), 0) == lax.broadcasted_iota(
        jnp.int32, (tile, tile), 1
    )


def stock_step(parts, tile, i, costs, dual, stock, eye, ones):
    new = []
    for r in range(parts):
        cost = spread_cost(costs[r][i : i + 1], eye, ones)
        change = cost - dual[(r - 1) % parts] + dual[r]
        new.append(jnp.maximum(stock[r] - STEP_PRIMAL * change, 0.0))
    return new


def first_stock_kernel(parts, size, tile, *refs):
    packets, stocks, combined = refs[:parts], refs[parts], refs[parts + 1 :]
    eye, ones = eye_of(tile), jnp.ones((tile, tile), BF)
    costs = [packets[r][2 * size :].astype(F32).astype(BF) for r in range(parts)]
    for i in range(size // tile):
        rows = slice(i * tile, (i + 1) * tile)
        behind = slice(size + i * tile, size + (i + 1) * tile)
        dual = [packets[r][rows].astype(F32) for r in range(parts)]
        stock = [packets[r][behind].astype(F32) for r in range(parts)]
        new = stock_step(parts, tile, i, costs, dual, stock, eye, ones)
        bar = [2.0 * new[r] - stock[r] for r in range(parts)]
        for r in range(parts):
            stocks[r, rows] = new[r]
            combined[r][rows] = (bar[(r + 1) % parts] - bar[r]).astype(BF)


def last_stock_kernel(parts, size, tile, *refs):
    packets, stocks, duals = refs[:parts], refs[parts], refs[parts + 1 : 2 * parts + 1]
    outs = refs[2 * parts + 1 :]
    eye, ones = eye_of(tile), jnp.ones((tile, tile), BF)
    costs = [packets[r][2 * size :].astype(F32).astype(BF) for r in range(parts)]
    for i in range(size // tile):
        rows = slice(i * tile, (i + 1) * tile)
        dual = [duals[r][rows].astype(F32) for r in range(parts)]
        stock = [stocks[r, rows] for r in range(parts)]
        new = stock_step(parts, tile, i, costs, dual, stock, eye, ones)
        bar = [2.0 * new[r] - stock[r] for r in range(parts)]
        for r in range(parts):
            outs[r][rows] = (bar[(r + 1) % parts] - bar[r]).astype(BF)
            outs[r][size + i * tile : size + (i + 1) * tile] = new[r].astype(BF)


def per_device(
    tiles,
    tile_row,
    tile_col,
    tile_live,
    block_place,
    demand,
    flow_cost,
    stock_cost,
    flows,
    stock,
    duals,
):
    unused_phases, slots, tile, unused_tile = tiles.shape
    scenarios = flows.shape[2]
    rows = duals.shape[1]
    parts = lax.axis_size("section")
    zones = lax.axis_size("zone")
    chips = zones // CORES
    blocks = block_place.shape[0]
    owned = blocks // zones
    band_tiles = rows // tile
    size = rows // parts
    shape = (chips, owned)
    tail = -(-(size // tile) // 16) * 16

    tiles = tiles.reshape(slots, tile, tile)
    duals2 = duals.reshape(rows, scenarios)
    stock2 = stock.reshape(rows, scenarios)
    flows2 = flows.reshape(owned * tile, scenarios)
    duals3 = duals.reshape(band_tiles, tile, scenarios)
    demand3 = demand.reshape(band_tiles, tile, scenarios)
    where = (tile_row, tile_col, tile_live, block_place)
    flops = 2 * slots * tile * tile * scenarios
    quarter = jax.ShapeDtypeStruct((size, scenarios), BF)
    quarter3 = jax.ShapeDtypeStruct((size // tile, tile, scenarios), BF)
    half_blocks = jax.ShapeDtypeStruct((blocks // 2, tile, scenarios), BF)
    pull_scratch = [
        pltpu.VMEM((band_tiles, tile, scenarios), BF),
        pltpu.VMEM((blocks + 1, tile, scenarios), F32),
    ]
    push_scratch = [
        pltpu.VMEM((blocks, tile, scenarios), BF),
        pltpu.VMEM((band_tiles + 1, tile, scenarios), F32),
    ]

    def collect(keep, send, others):
        both = (keep.astype(F32) + swap_core(send).astype(F32)).astype(BF)
        parts_of = [both[k * owned : (k + 1) * owned] for k in range(chips)]
        got = [rotate_chip(parts_of[k], k) for k in range(1, chips)]
        got = after(got, others)
        total = parts_of[0].astype(F32)
        for value in got:
            total = total + value.astype(F32)
        return total.reshape(owned * tile, scenarios)

    def spread(value, others):
        own = [rotate_chip(value, k) for k in range(1, chips)]
        own = after(own, others)
        near = jnp.concatenate([value, *own], axis=0).reshape(blocks // 2, tile, scenarios)
        return near, swap_core(near)

    def step_flows(now, pulled):
        new = jnp.maximum(now - STEP_PRIMAL * (flow_cost[0][:, None] - pulled), 0.0)
        return new, ((2.0 * new - now).astype(BF) * BF(-STEP_DUAL))

    ins = (tile_row, tile_col, tile_live, block_place, tiles, duals2, stock2, stock_cost)
    keep, send, *packets = pl.pallas_call(
        functools.partial(pull_kernel, shape, parts, size),
        out_shape=[half_blocks, half_blocks]
        + [jax.ShapeDtypeStruct((2 * size + tail, scenarios), BF)] * parts,
        in_specs=[pl.BlockSpec(memory_space=pltpu.HBM)] * len(ins),
        out_specs=[VMEM] * 2 + [pl.BlockSpec(memory_space=pltpu.HBM)] * parts,
        scratch_shapes=[pltpu.SMEM(v.shape, v.dtype) for v in ins[:4]]
        + [pltpu.VMEM(v.shape, v.dtype) for v in ins[4:]]
        + [pltpu.VMEM((2 * size + tail, scenarios), BF)] * parts
        + pull_scratch
        + [pltpu.SemaphoreType.DMA((len(ins),)), pltpu.SemaphoreType.DMA((parts,))],
        compiler_params=pltpu.CompilerParams(vmem_limit_bytes=FULL),
        cost_estimate=pl.CostEstimate(
            flops=flops, bytes_accessed=12 * rows * scenarios, transcendentals=0
        ),
    )(*ins)
    packets = [packets[0]] + [rotate(packets[r], "section", r) for r in range(1, parts)]

    stocks, *combined = call(
        functools.partial(first_stock_kernel, parts, size, tile),
        [jax.ShapeDtypeStruct((parts, size, scenarios), F32)] + [quarter] * parts,
        [],
        STEP_COST,
        10 * rows * scenarios,
        *packets,
    )
    pulled = collect(keep, send, combined)
    flows1, bar1 = step_flows(flows2, pulled)
    combined = [combined[0]] + [rotate(combined[r], "section", -r) for r in range(1, parts)]
    near, far = spread(bar1, combined)
    combined = [c.reshape(size // tile, tile, scenarios) for c in combined]

    duals1, keep, send, *halves = call(
        functools.partial(push_pull_kernel, shape, parts, size),
        [jax.ShapeDtypeStruct((band_tiles, tile, scenarios), F32), half_blocks, half_blocks]
        + [quarter3] * parts,
        [push_scratch[0], pull_scratch[0], push_scratch[1], pull_scratch[1]],
        2 * flops,
        16 * rows * scenarios + 2 * slots * tile * tile,
        *where,
        tiles,
        duals3,
        demand3,
        near,
        far,
        *combined,
        smem=4,
    )
    halves = [h.reshape(size, scenarios) for h in halves]
    halves = [halves[0]] + [rotate(halves[r], "section", r) for r in range(1, parts)]
    outs = call(
        functools.partial(last_stock_kernel, parts, size, tile),
        [jax.ShapeDtypeStruct((2 * size, scenarios), BF)] * parts,
        [],
        STEP_COST,
        10 * rows * scenarios,
        *packets,
        stocks,
        *halves,
    )
    pulled = collect(keep, send, outs)
    flows2_out, bar2 = step_flows(flows1, pulled)
    outs = [outs[0]] + [rotate(outs[r], "section", -r) for r in range(1, parts)]
    near, far = spread(bar2, outs)
    base = call(
        functools.partial(push_kernel, shape),
        jax.ShapeDtypeStruct((band_tiles, tile, scenarios), F32),
        push_scratch,
        flops,
        12 * rows * scenarios + 2 * slots * tile * tile,
        *where,
        tiles,
        duals1,
        demand3,
        near,
        far,
        smem=4,
    )
    whole = jax.ShapeDtypeStruct((rows, scenarios), F32)
    duals_out, stock_out = pl.pallas_call(
        functools.partial(final_kernel, parts, size),
        out_shape=[whole, whole],
        in_specs=[VMEM] * (parts + 1),
        out_specs=[pl.BlockSpec(memory_space=pltpu.HBM)] * 2,
        scratch_shapes=[pltpu.VMEM((rows, scenarios), F32)] * 2
        + [pltpu.SemaphoreType.DMA((2 * parts,))],
        compiler_params=pltpu.CompilerParams(vmem_limit_bytes=LIMIT),
        cost_estimate=pl.CostEstimate(
            flops=0, bytes_accessed=12 * rows * scenarios, transcendentals=0
        ),
    )(base.reshape(rows, scenarios), *outs)
    return (
        flows2_out.reshape(flows.shape),
        stock_out.reshape(stock.shape),
        duals_out.reshape(duals.shape),
    )


def solution(mesh):
    in_specs = (
        P("section", "zone", None, None),
        P("section", "zone"),
        P("section", "zone"),
        P("section", "zone"),
        P(),
        P("section", "zone", None),
        P("section", "zone"),
        P("section", "zone"),
        P("section", "zone", None),
        P("section", "zone", None),
        P("section", "zone", None),
    )
    out_specs = (P("section", "zone", None), P("section", "zone", None), P("section", "zone", None))
    return jax.shard_map(
        per_device, mesh=mesh, in_specs=in_specs, out_specs=out_specs, check_vma=False
    )
```

```python
import functools

import jax
import jax.numpy as jnp
from jax import lax
from jax.experimental import pallas as pl
from jax.experimental.pallas import tpu as pltpu
from jax.sharding import PartitionSpec as P

ITERS = 2

STEP_PRIMAL = 0.25
STEP_DUAL = 0.25

BF = jnp.bfloat16
F32 = jnp.float32
VMEM = pl.BlockSpec(memory_space=pltpu.VMEM)
SMEM = pl.BlockSpec(memory_space=pltpu.SMEM)
LIMIT = 48 * 1024 * 1024
FULL = 62 * 1024 * 1024
CORES = 2
STEP_COST = 0


def rotate(value, axis, by):
    size = lax.axis_size(axis)
    return lax.ppermute(value, axis, [(i, (i + by) % size) for i in range(size)])


def rotate_chip(value, by):
    size = lax.axis_size("zone")
    return lax.ppermute(value, "zone", [(i, (i + by * CORES) % size) for i in range(size)])


def flip_chip(value, by):
    size = lax.axis_size("zone")
    return lax.ppermute(value, "zone", [(i, i ^ (by * CORES)) for i in range(size)])


def swap_core(value):
    size = lax.axis_size("zone")
    return lax.ppermute(value, "zone", [(i, i ^ 1) for i in range(size)])


def after(values, others):
    return lax.optimization_barrier((*values, *others))[: len(values)]


def call(kernel, outs, scratch, flops, moved, *args, smem=0):
    return pl.pallas_call(
        kernel,
        out_shape=outs,
        in_specs=[SMEM] * smem + [VMEM] * (len(args) - smem),
        out_specs=jax.tree.map(lambda _: VMEM, outs),
        scratch_shapes=scratch,
        compiler_params=pltpu.CompilerParams(vmem_limit_bytes=LIMIT),
        cost_estimate=pl.CostEstimate(flops=flops, bytes_accessed=moved, transcendentals=0),
    )(*args)


def quarter_rows(by, parts, size):
    part = lax.rem(lax.axis_index("section") + by, parts)
    return pl.ds(pl.multiple_of(part * size, size), size)


def pack_kernel(parts, size, *refs):
    duals_in, stock_in, cost_in = refs[:3]
    outs = refs[3 : 2 + parts]
    duals, stock, cost = refs[2 + parts : 5 + parts]
    packets = refs[5 + parts : 4 + 2 * parts]
    sems, cost_sem, out_sems = refs[4 + 2 * parts :]
    tile = packets[0].shape[1]
    pieces = size // tile
    cost_copy = pltpu.make_async_copy(cost_in, cost, cost_sem)
    cost_copy.start()
    gets, gives = [], []
    for r in range(1, parts):
        rows = quarter_rows(r, parts, size)
        here = pl.ds((r - 1) * size, size)
        for i, (there, held) in enumerate(((duals_in, duals), (stock_in, stock))):
            gets.append(
                pltpu.make_async_copy(there.at[rows], held.at[here], sems.at[2 * (r - 1) + i])
            )
            gets[-1].start()
        gives.append(pltpu.make_async_copy(packets[r - 1], outs[r - 1], out_sems.at[r - 1]))
    cost_copy.wait()
    for r in range(1, parts):
        part = lax.rem(lax.axis_index("section") + r, parts)
        packet = packets[r - 1]
        here = slice((r - 1) * size, r * size)
        tail = packet.shape[0] - 2 * size
        lines = [
            cost[:, pl.ds(pl.multiple_of(part * size + i * tile, tile), tile)]
            for i in range(pieces)
        ]
        lines.append(jnp.zeros((tail - pieces, tile), F32))
        packet[2 * size :] = jnp.concatenate(lines, axis=0).astype(BF)
        gets[2 * r - 2].wait()
        packet[0:size] = duals[here].astype(BF)
        gets[2 * r - 1].wait()
        packet[size : 2 * size] = stock[here].astype(BF)
        gives[r - 1].start()
    for give in gives:
        give.wait()


def block_slot(place, col, k, shape):
    chips, owned = shape
    zone = lax.axis_index("zone")
    chip, core = lax.div(zone, CORES), lax.rem(zone, CORES)
    position = place[col[0, k]]
    owner, inner = lax.div(position, owned), lax.rem(position, owned)
    differ = lax.div(owner, CORES) ^ chip
    away, step, bit = 0, chips // 2, 1
    while step:
        away = away + bit * lax.rem(lax.div(differ, step), 2)
        step, bit = step // 2, bit * 2
    half = jnp.where(lax.rem(owner, CORES) == core, 0, chips * owned)
    return half + away * owned + inner


def pull_slots(shape, row, col, live, place, tiles, half, acc):
    slots = tiles.shape[0]
    blocks = acc.shape[0] - 1
    acc[...] = jnp.zeros_like(acc)

    def step(k, carry):
        there = jnp.where(live[0, k] == 1, block_slot(place, col, k, shape), blocks)
        acc[there] += lax.dot_general(
            tiles[k], half[row[0, k]], (((0,), (0,)), ((), ())), preferred_element_type=F32
        )
        return carry

    lax.fori_loop(0, slots, step, 0, unroll=8)


def push_slots(shape, row, col, live, place, tiles, blocks, acc):
    slots = tiles.shape[0]
    spare = acc.shape[0] - 1

    def step(k, carry):
        there = jnp.where(live[0, k] == 1, row[0, k], spare)
        acc[there] += jnp.dot(
            tiles[k],
            blocks[block_slot(place, col, k, shape)],
            preferred_element_type=F32,
        )
        return carry

    lax.fori_loop(0, slots, step, 0, unroll=8)


def give_partials(acc, keep, send):
    n = keep.shape[0]
    keep[...] = acc[0:n].astype(BF)
    send[...] = acc[n : 2 * n].astype(BF)


def pull_kernel(shape, row, col, live, place, tiles, duals, keep, send, *scratch):
    half, acc = scratch if len(scratch) == 2 else (duals, scratch[0])
    if len(scratch) == 2:
        half[...] = duals[...].astype(BF)
    pull_slots(shape, row, col, live, place, tiles, half, acc)
    give_partials(acc, keep, send)


def step_duals(shape, parts, size, refs, blocks, acc):
    row, col, live, place, tiles, duals, demand, near, far = refs[:9]
    combined = refs[9:]
    n = near.shape[0]
    blocks[0:n] = near[...]
    blocks[n : 2 * n] = far[...]
    pieces = size // tiles.shape[1]
    for r in range(parts):
        part = lax.rem(lax.axis_index("section") + r, parts)
        rows = pl.ds(part * pieces, pieces)
        acc[rows] = (
            duals[rows]
            + (STEP_DUAL * 0.25) * demand[rows].astype(F32)
            - STEP_DUAL * combined[r][0:size].astype(F32).reshape(pieces, *duals.shape[1:])
        )
    push_slots(shape, row, col, live, place, tiles, blocks, acc)


def push_step_kernel(shape, parts, size, *refs):
    ins, (next_duals, half), packets = refs[: 9 + parts], refs[9 + parts : 11 + parts], refs[11 + parts : -2]
    blocks, acc = refs[-2:]
    tile = ins[4].shape[1]
    step_duals(shape, parts, size, ins, blocks, acc)
    n = next_duals.shape[0]
    next_duals[...] = acc[0:n]
    half[...] = acc[0:n].astype(BF)
    pieces = size // tile
    for r in range(1, parts):
        part = lax.rem(lax.axis_index("section") + r, parts)
        packets[r - 1][...] = half[pl.ds(part * pieces, pieces)]


def place_kernel(parts, size, *refs):
    out = refs[parts]
    for r in range(parts):
        out[quarter_rows(r, parts, size), :] = refs[r][size:].astype(F32)


def last_push_kernel(shape, parts, size, *refs):
    ins = refs[: 9 + parts]
    next_duals, blocks, acc = refs[9 + parts :]
    step_duals(shape, parts, size, ins, blocks, acc)
    next_duals[...] = acc[0 : next_duals.shape[0]]


def own_rows(size, tile, i):
    return pl.ds(pl.multiple_of(lax.axis_index("section") * size + i * tile, tile), tile)


def eye_of(tile):
    return lax.broadcasted_iota(jnp.int32, (tile, tile), 0) == lax.broadcasted_iota(
        jnp.int32, (tile, tile), 1
    )


def stock_step(parts, lines, dual, stock, eye, ones):
    new = []
    for r in range(parts):
        line = jnp.where(eye, lines[r], 0.0).astype(BF)
        cost = jnp.dot(line, ones, preferred_element_type=F32)
        change = cost - dual[(r - 1) % parts] + dual[r]
        new.append(jnp.maximum(stock[r] - STEP_PRIMAL * change, 0.0))
    return new


def first_stock_kernel(parts, size, tile, *refs):
    own_duals, own_stock, own_cost, packets = *refs[:3], refs[3 : 2 + parts]
    stocks, combined = refs[2 + parts], refs[3 + parts :]
    eye, ones = eye_of(tile), jnp.ones((tile, tile), BF)
    costs = [None] + [packet[2 * size :].astype(F32) for packet in packets]
    for i in range(size // tile):
        rows = slice(i * tile, (i + 1) * tile)
        behind = slice(size + i * tile, size + (i + 1) * tile)
        own = own_rows(size, tile, i)
        dual = [own_duals[own, :]] + [packet[rows].astype(F32) for packet in packets]
        stock = [own_stock[own, :]] + [packet[behind].astype(F32) for packet in packets]
        lines = [own_cost[:, own]] + [c[i : i + 1] for c in costs[1:]]
        new = stock_step(parts, lines, dual, stock, eye, ones)
        bar = [2.0 * new[r] - stock[r] for r in range(parts)]
        for r in range(parts):
            stocks[r, rows] = new[r]
            combined[r][rows] = (bar[(r + 1) % parts] - bar[r]).astype(BF)


def last_stock_kernel(parts, size, tile, *refs):
    own_duals, own_cost, packets = *refs[:2], refs[2 : 1 + parts]
    stocks, duals, outs = refs[1 + parts], refs[2 + parts : 1 + 2 * parts], refs[1 + 2 * parts :]
    eye, ones = eye_of(tile), jnp.ones((tile, tile), BF)
    costs = [None] + [packet[2 * size :].astype(F32) for packet in packets]
    for i in range(size // tile):
        rows = slice(i * tile, (i + 1) * tile)
        behind = slice(size + i * tile, size + (i + 1) * tile)
        own = own_rows(size, tile, i)
        dual = [own_duals[own, :]] + [d[rows].astype(F32) for d in duals]
        stock = [stocks[r, rows] for r in range(parts)]
        lines = [own_cost[:, own]] + [c[i : i + 1] for c in costs[1:]]
        new = stock_step(parts, lines, dual, stock, eye, ones)
        bar = [2.0 * new[r] - stock[r] for r in range(parts)]
        for r in range(parts):
            outs[r][rows] = (bar[(r + 1) % parts] - bar[r]).astype(BF)
            outs[r][behind] = new[r].astype(BF)


def per_device(
    tiles,
    tile_row,
    tile_col,
    tile_live,
    block_place,
    demand,
    flow_cost,
    stock_cost,
    flows,
    stock,
    duals,
):
    unused_phases, slots, tile, unused_tile = tiles.shape
    scenarios = flows.shape[2]
    rows = duals.shape[1]
    parts = lax.axis_size("section")
    zones = lax.axis_size("zone")
    chips = zones // CORES
    blocks = block_place.shape[0]
    owned = blocks // zones
    band_tiles = rows // tile
    size = rows // parts
    shape = (chips, owned)
    tail = -(-(size // tile) // 16) * 16

    tiles = tiles.reshape(slots, tile, tile)
    duals2 = duals.reshape(rows, scenarios)
    stock2 = stock.reshape(rows, scenarios)
    flows2 = flows.reshape(owned * tile, scenarios)
    duals3 = duals.reshape(band_tiles, tile, scenarios)
    demand3 = demand.reshape(band_tiles, tile, scenarios)
    where = (tile_row, tile_col, tile_live, block_place)
    flops = 2 * slots * tile * tile * scenarios
    quarter = jax.ShapeDtypeStruct((size, scenarios), BF)
    quarter3 = jax.ShapeDtypeStruct((size // tile, tile, scenarios), BF)
    whole_half = jax.ShapeDtypeStruct((band_tiles, tile, scenarios), BF)
    half_blocks = jax.ShapeDtypeStruct((blocks // 2, tile, scenarios), BF)
    pull_scratch = [
        pltpu.VMEM((band_tiles, tile, scenarios), BF),
        pltpu.VMEM((blocks + 1, tile, scenarios), F32),
    ]
    push_scratch = [
        pltpu.VMEM((blocks, tile, scenarios), BF),
        pltpu.VMEM((band_tiles + 1, tile, scenarios), F32),
    ]

    known = block_place[0] >= 0

    def apart(f, *args):
        shapes = jax.eval_shape(f, *args)

        def none(*unused):
            return jax.tree.map(lambda v: jnp.zeros(v.shape, v.dtype), shapes)

        return lax.cond(known, f, none, *args)

    def add(value, other):
        return value.astype(F32) + other.astype(F32)

    def collect(keep, send, others):
        both = add(keep, send).astype(BF)
        parts_of = [both[k * owned : (k + 1) * owned] for k in range(chips)]
        got = []
        for k in range(1, chips):
            away = sum((chips // 2 >> i) * ((k >> i) & 1) for i in range(chips.bit_length()))
            got.append(flip_chip(parts_of[k], away))
        got = after(got, others)
        total = parts_of[0].astype(F32)
        for value in got:
            total = total + value.astype(F32)
        return total.reshape(owned * tile, scenarios)

    def spread(value, others):
        own = [value]
        step = chips // 2
        while step:
            own = own + [flip_chip(v, step) for v in own]
            step //= 2
        own = own[1:]
        own = after(own, others)
        near = jnp.concatenate([value, *own], axis=0).reshape(blocks // 2, tile, scenarios)
        return near, swap_core(near)

    def step_flows(now, pulled):
        new = jnp.maximum(now - STEP_PRIMAL * (flow_cost[0][:, None] - pulled), 0.0)
        return new, ((2.0 * new - now).astype(BF) * BF(-STEP_DUAL))

    ins = (duals2, stock2, stock_cost)
    packed = [jax.ShapeDtypeStruct((2 * size + tail, scenarios), BF)] * (parts - 1)
    packets = pl.pallas_call(
        functools.partial(pack_kernel, parts, size),
        out_shape=packed,
        in_specs=[pl.BlockSpec(memory_space=pltpu.HBM)] * len(ins),
        out_specs=[pl.BlockSpec(memory_space=pltpu.HBM)] * len(packed),
        scratch_shapes=[
            pltpu.VMEM(((parts - 1) * size, scenarios), F32),
            pltpu.VMEM(((parts - 1) * size, scenarios), F32),
            pltpu.VMEM(stock_cost.shape, F32),
        ]
        + [pltpu.VMEM(v.shape, v.dtype) for v in packed]
        + [
            pltpu.SemaphoreType.DMA((2 * (parts - 1),)),
            pltpu.SemaphoreType.DMA(()),
            pltpu.SemaphoreType.DMA((parts - 1,)),
        ],
        compiler_params=pltpu.CompilerParams(vmem_limit_bytes=FULL),
        cost_estimate=pl.CostEstimate(
            flops=0, bytes_accessed=12 * rows * scenarios, transcendentals=0
        ),
    )(*ins)
    packets = [rotate(packets[r - 1], "section", r) for r in range(1, parts)]

    stocks, *combined = call(
        functools.partial(first_stock_kernel, parts, size, tile),
        [jax.ShapeDtypeStruct((parts, size, scenarios), F32)] + [quarter] * parts,
        [],
        0,
        10 * rows * scenarios,
        duals2,
        stock2,
        stock_cost,
        *packets,
    )

    def pull(value, scratch):
        keep, send = call(
            functools.partial(pull_kernel, shape),
            [half_blocks, half_blocks],
            scratch,
            flops,
            2 * rows * scenarios + 2 * slots * tile * tile,
            *where,
            tiles,
            value,
            smem=4,
        )
        return keep, swap_core(send)

    keep, send = apart(lambda value: pull(value, pull_scratch), duals3)
    pulled = collect(keep, send, combined)
    flows1, bar1 = step_flows(flows2, pulled)
    combined = [combined[0]] + [rotate(combined[r], "section", -r) for r in range(1, parts)]
    near, far = spread(bar1, combined)

    duals1, half, *halves = call(
        functools.partial(push_step_kernel, shape, parts, size),
        [jax.ShapeDtypeStruct((band_tiles, tile, scenarios), F32), whole_half]
        + [quarter3] * (parts - 1),
        push_scratch,
        flops,
        16 * rows * scenarios + 2 * slots * tile * tile,
        *where,
        tiles,
        duals3,
        demand3,
        near,
        far,
        *combined,
        smem=4,
    )
    halves = [rotate(halves[r - 1].reshape(size, scenarios), "section", r) for r in range(1, parts)]
    outs = call(
        functools.partial(last_stock_kernel, parts, size, tile),
        [jax.ShapeDtypeStruct((2 * size, scenarios), BF)] * parts,
        [],
        0,
        10 * rows * scenarios,
        duals1.reshape(rows, scenarios),
        stock_cost,
        *packets,
        stocks,
        *halves,
    )
    keep, send = pull(half, pull_scratch[1:])
    pulled = collect(keep, send, outs)
    outs = [outs[0]] + [rotate(outs[r], "section", -r) for r in range(1, parts)]
    flows2_out, bar2 = step_flows(flows1, pulled)
    near, far = spread(bar2, outs)
    duals_out = call(
        functools.partial(last_push_kernel, shape, parts, size),
        jax.ShapeDtypeStruct((band_tiles, tile, scenarios), F32),
        push_scratch,
        flops,
        14 * rows * scenarios + 2 * slots * tile * tile,
        *where,
        tiles,
        duals1,
        demand3,
        near,
        far,
        *outs,
        smem=4,
    )
    stock_out = call(
        functools.partial(place_kernel, parts, size),
        jax.ShapeDtypeStruct((rows, scenarios), F32),
        [],
        0,
        6 * rows * scenarios,
        *outs,
    )
    return (
        flows2_out.reshape(flows.shape),
        stock_out.reshape(stock.shape),
        duals_out.reshape(duals.shape),
    )


def solution(mesh):
    in_specs = (
        P("section", "zone", None, None),
        P("section", "zone"),
        P("section", "zone"),
        P("section", "zone"),
        P(),
        P("section", "zone", None),
        P("section", "zone"),
        P("section", "zone"),
        P("section", "zone", None),
        P("section", "zone", None),
        P("section", "zone", None),
    )
    out_specs = (P("section", "zone", None), P("section", "zone", None), P("section", "zone", None))
    return jax.shard_map(
        per_device, mesh=mesh, in_specs=in_specs, out_specs=out_specs, check_vma=False
    )
```

```python
import functools

import jax
import jax.numpy as jnp
from jax import lax
from jax.experimental import pallas as pl
from jax.experimental.pallas import tpu as pltpu
from jax.sharding import PartitionSpec as P

ITERS = 2

STEP_PRIMAL = 0.25
STEP_DUAL = 0.25

BF = jnp.bfloat16
F32 = jnp.float32
VMEM = pl.BlockSpec(memory_space=pltpu.VMEM)
SMEM = pl.BlockSpec(memory_space=pltpu.SMEM)
LIMIT = 48 * 1024 * 1024
FULL = 62 * 1024 * 1024
CORES = 2
STEP_COST = 0


def rotate(value, axis, by):
    size = lax.axis_size(axis)
    return lax.ppermute(value, axis, [(i, (i + by) % size) for i in range(size)])


def rotate_chip(value, by):
    size = lax.axis_size("zone")
    return lax.ppermute(value, "zone", [(i, (i + by * CORES) % size) for i in range(size)])


def flip_chip(value, by):
    size = lax.axis_size("zone")
    return lax.ppermute(value, "zone", [(i, i ^ (by * CORES)) for i in range(size)])


def swap_core(value):
    size = lax.axis_size("zone")
    return lax.ppermute(value, "zone", [(i, i ^ 1) for i in range(size)])


def after(values, others):
    return lax.optimization_barrier((*values, *others))[: len(values)]


def call(kernel, outs, scratch, flops, moved, *args, smem=0, spec=VMEM):
    return pl.pallas_call(
        kernel,
        out_shape=outs,
        in_specs=[SMEM] * smem + [VMEM] * (len(args) - smem),
        out_specs=jax.tree.map(lambda _: spec, outs),
        scratch_shapes=scratch,
        compiler_params=pltpu.CompilerParams(vmem_limit_bytes=LIMIT),
        cost_estimate=pl.CostEstimate(flops=flops, bytes_accessed=moved, transcendentals=0),
    )(*args)


def quarter_rows(by, parts, size):
    part = lax.rem(lax.axis_index("section") + by, parts)
    return pl.ds(pl.multiple_of(part * size, size), size)


def pack_kernel(parts, size, *refs):
    duals_in, stock_in, cost_in = refs[:3]
    outs = refs[3 : 2 + parts]
    duals, stock, cost = refs[2 + parts : 5 + parts]
    packets = refs[5 + parts : 4 + 2 * parts]
    sems, cost_sem, out_sems = refs[4 + 2 * parts :]
    tile = packets[0].shape[1]
    pieces = size // tile
    cost_copy = pltpu.make_async_copy(cost_in, cost, cost_sem)
    cost_copy.start()
    gets, gives = [], []
    for r in range(1, parts):
        rows = quarter_rows(r, parts, size)
        here = pl.ds((r - 1) * size, size)
        for i, (there, held) in enumerate(((duals_in, duals), (stock_in, stock))):
            gets.append(
                pltpu.make_async_copy(there.at[rows], held.at[here], sems.at[2 * (r - 1) + i])
            )
            gets[-1].start()
        gives.append(pltpu.make_async_copy(packets[r - 1], outs[r - 1], out_sems.at[r - 1]))
    cost_copy.wait()
    for r in range(1, parts):
        part = lax.rem(lax.axis_index("section") + r, parts)
        packet = packets[r - 1]
        here = slice((r - 1) * size, r * size)
        tail = packet.shape[0] - 2 * size
        lines = [
            cost[:, pl.ds(pl.multiple_of(part * size + i * tile, tile), tile)]
            for i in range(pieces)
        ]
        lines.append(jnp.zeros((tail - pieces, tile), F32))
        packet[2 * size :] = jnp.concatenate(lines, axis=0).astype(BF)
        gets[2 * r - 2].wait()
        packet[0:size] = duals[here].astype(BF)
        gets[2 * r - 1].wait()
        packet[size : 2 * size] = stock[here].astype(BF)
        gives[r - 1].start()
    for give in gives:
        give.wait()


def block_slot(place, col, k, shape):
    chips, owned = shape
    zone = lax.axis_index("zone")
    chip, core = lax.div(zone, CORES), lax.rem(zone, CORES)
    position = place[col[0, k]]
    owner, inner = lax.div(position, owned), lax.rem(position, owned)
    differ = lax.div(owner, CORES) ^ chip
    away, step, bit = 0, chips // 2, 1
    while step:
        away = away + bit * lax.rem(lax.div(differ, step), 2)
        step, bit = step // 2, bit * 2
    half = jnp.where(lax.rem(owner, CORES) == core, 0, chips * owned)
    return half + away * owned + inner


def list_slots(shape, rows, row, col, live, place, slots):
    def step(k, carry):
        block = block_slot(place, col, k, shape)
        alive = live[0, k] == 1
        slots[0, k] = block
        slots[1, k] = jnp.where(alive, block, CORES * shape[0] * shape[1])
        slots[2, k] = row[0, k]
        slots[3, k] = jnp.where(alive, row[0, k], rows)
        return carry

    lax.fori_loop(0, slots.shape[1], step, 0)


def pull_slots(slots, tiles, half, acc):
    acc[...] = jnp.zeros_like(acc)

    def step(k, carry):
        acc[slots[1, k]] += lax.dot_general(
            tiles[k], half[slots[2, k]], (((0,), (0,)), ((), ())), preferred_element_type=F32
        )
        return carry

    lax.fori_loop(0, tiles.shape[0], step, 0, unroll=min(32, tiles.shape[0]))


def push_slots(slots, tiles, blocks, acc):
    def step(k, carry):
        acc[slots[3, k]] += jnp.dot(
            tiles[k], blocks[slots[0, k]], preferred_element_type=F32
        )
        return carry

    lax.fori_loop(0, tiles.shape[0], step, 0, unroll=min(32, tiles.shape[0]))


def give_partials(acc, keep, send):
    n = keep.shape[0]
    keep[...] = acc[0:n].astype(BF)
    send[...] = acc[n : 2 * n].astype(BF)


def first_pull_kernel(shape, row, col, live, place, tiles, duals, keep, send, slots, half, acc):
    list_slots(shape, duals.shape[0], row, col, live, place, slots)
    half[...] = duals[...].astype(BF)
    pull_slots(slots, tiles, half, acc)
    give_partials(acc, keep, send)


def pull_kernel(slots, tiles, half, keep, send, acc):
    pull_slots(slots, tiles, half, acc)
    give_partials(acc, keep, send)


def step_duals(parts, size, refs, blocks, acc):
    slots, tiles, duals, demand, near, far = refs[:6]
    combined = refs[6:]
    n = near.shape[0]
    blocks[0:n] = near[...]
    blocks[n : 2 * n] = far[...]
    pieces = size // tiles.shape[1]
    for r in range(parts):
        part = lax.rem(lax.axis_index("section") + r, parts)
        rows = pl.ds(part * pieces, pieces)
        acc[rows] = (
            duals[rows]
            + (STEP_DUAL * 0.25) * demand[rows].astype(F32)
            - STEP_DUAL * combined[r][0:size].astype(F32).reshape(pieces, *duals.shape[1:])
        )
    push_slots(slots, tiles, blocks, acc)


def push_step_kernel(parts, size, *refs):
    ins, next_duals, half = refs[: 6 + parts], refs[6 + parts], refs[7 + parts]
    packets, blocks, acc = refs[8 + parts : -2], refs[-2], refs[-1]
    tile = ins[1].shape[1]
    step_duals(parts, size, ins, blocks, acc)
    n = next_duals.shape[0]
    next_duals[...] = acc[0:n]
    half[...] = acc[0:n].astype(BF)
    pieces = size // tile
    for r in range(1, parts):
        part = lax.rem(lax.axis_index("section") + r, parts)
        packets[r - 1][...] = half[pl.ds(part * pieces, pieces)]


def place_kernel(parts, size, *refs):
    out = refs[parts]
    for r in range(parts):
        out[quarter_rows(r, parts, size), :] = refs[r][size:].astype(F32)


def last_push_kernel(parts, size, *refs):
    ins = refs[: 6 + parts]
    next_duals, blocks, acc, sem = refs[6 + parts :]
    step_duals(parts, size, ins, blocks, acc)
    copy = pltpu.make_async_copy(acc.at[pl.ds(0, next_duals.shape[0])], next_duals, sem)
    copy.start()
    copy.wait()


def own_rows(size, tile, i):
    return pl.ds(pl.multiple_of(lax.axis_index("section") * size + i * tile, tile), tile)


def eye_of(tile):
    return lax.broadcasted_iota(jnp.int32, (tile, tile), 0) == lax.broadcasted_iota(
        jnp.int32, (tile, tile), 1
    )


def stock_step(parts, lines, dual, stock, eye, ones):
    new = []
    for r in range(parts):
        line = jnp.where(eye, lines[r], 0.0).astype(BF)
        cost = jnp.dot(line, ones, preferred_element_type=F32)
        change = cost - dual[(r - 1) % parts] + dual[r]
        new.append(jnp.maximum(stock[r] - STEP_PRIMAL * change, 0.0))
    return new


def first_stock_kernel(parts, size, tile, *refs):
    own_duals, own_stock, own_cost, packets = *refs[:3], refs[3 : 2 + parts]
    stocks, combined = refs[2 + parts], refs[3 + parts :]
    eye, ones = eye_of(tile), jnp.ones((tile, tile), BF)
    costs = [None] + [packet[2 * size :].astype(F32) for packet in packets]
    for i in range(size // tile):
        rows = slice(i * tile, (i + 1) * tile)
        behind = slice(size + i * tile, size + (i + 1) * tile)
        own = own_rows(size, tile, i)
        dual = [own_duals[own, :]] + [packet[rows].astype(F32) for packet in packets]
        stock = [own_stock[own, :]] + [packet[behind].astype(F32) for packet in packets]
        lines = [own_cost[:, own]] + [c[i : i + 1] for c in costs[1:]]
        new = stock_step(parts, lines, dual, stock, eye, ones)
        bar = [2.0 * new[r] - stock[r] for r in range(parts)]
        for r in range(parts):
            stocks[r, rows] = new[r]
            combined[r][rows] = (bar[(r + 1) % parts] - bar[r]).astype(BF)


def last_stock_kernel(parts, size, tile, *refs):
    own_duals, own_cost, packets = *refs[:2], refs[2 : 1 + parts]
    stocks, duals, outs = refs[1 + parts], refs[2 + parts : 1 + 2 * parts], refs[1 + 2 * parts :]
    eye, ones = eye_of(tile), jnp.ones((tile, tile), BF)
    costs = [None] + [packet[2 * size :].astype(F32) for packet in packets]
    for i in range(size // tile):
        rows = slice(i * tile, (i + 1) * tile)
        behind = slice(size + i * tile, size + (i + 1) * tile)
        own = own_rows(size, tile, i)
        dual = [own_duals[own, :]] + [d[rows].astype(F32) for d in duals]
        stock = [stocks[r, rows] for r in range(parts)]
        lines = [own_cost[:, own]] + [c[i : i + 1] for c in costs[1:]]
        new = stock_step(parts, lines, dual, stock, eye, ones)
        bar = [2.0 * new[r] - stock[r] for r in range(parts)]
        for r in range(parts):
            outs[r][rows] = (bar[(r + 1) % parts] - bar[r]).astype(BF)
            outs[r][behind] = new[r].astype(BF)


def per_device(
    tiles,
    tile_row,
    tile_col,
    tile_live,
    block_place,
    demand,
    flow_cost,
    stock_cost,
    flows,
    stock,
    duals,
):
    unused_phases, slots, tile, unused_tile = tiles.shape
    scenarios = flows.shape[2]
    rows = duals.shape[1]
    parts = lax.axis_size("section")
    zones = lax.axis_size("zone")
    chips = zones // CORES
    blocks = block_place.shape[0]
    owned = blocks // zones
    band_tiles = rows // tile
    size = rows // parts
    shape = (chips, owned)
    tail = -(-(size // tile) // 16) * 16

    tiles = tiles.reshape(slots, tile, tile)
    duals2 = duals.reshape(rows, scenarios)
    stock2 = stock.reshape(rows, scenarios)
    flows2 = flows.reshape(owned * tile, scenarios)
    duals3 = duals.reshape(band_tiles, tile, scenarios)
    demand3 = demand.reshape(band_tiles, tile, scenarios)
    flops = 2 * slots * tile * tile * scenarios
    quarter = jax.ShapeDtypeStruct((size, scenarios), BF)
    quarter3 = jax.ShapeDtypeStruct((size // tile, tile, scenarios), BF)
    whole_half = jax.ShapeDtypeStruct((band_tiles, tile, scenarios), BF)
    half_blocks = jax.ShapeDtypeStruct((blocks // 2, tile, scenarios), BF)
    pull_scratch = [
        pltpu.VMEM((band_tiles, tile, scenarios), BF),
        pltpu.VMEM((blocks + 1, tile, scenarios), F32),
    ]
    push_scratch = [
        pltpu.VMEM((blocks, tile, scenarios), BF),
        pltpu.VMEM((band_tiles + 1, tile, scenarios), F32),
    ]

    known = block_place[0] >= 0

    def apart(f, *args):
        shapes = jax.eval_shape(f, *args)

        def none(*unused):
            return jax.tree.map(lambda v: jnp.zeros(v.shape, v.dtype), shapes)

        return lax.cond(known, f, none, *args)

    def add(value, other):
        return value.astype(F32) + other.astype(F32)

    def collect(keep, send, others):
        both = add(keep, send).astype(BF)
        parts_of = [both[k * owned : (k + 1) * owned] for k in range(chips)]
        got = []
        for k in range(1, chips):
            away = sum((chips // 2 >> i) * ((k >> i) & 1) for i in range(chips.bit_length()))
            got.append(flip_chip(parts_of[k], away))
        got = after(got, others)
        total = parts_of[0].astype(F32)
        for value in got:
            total = total + value.astype(F32)
        return total.reshape(owned * tile, scenarios)

    def spread(value, others):
        own = [value]
        step = chips // 2
        while step:
            own = own + [flip_chip(v, step) for v in own]
            step //= 2
        own = own[1:]
        own = after(own, others)
        near = jnp.concatenate([value, *own], axis=0).reshape(blocks // 2, tile, scenarios)
        return near, swap_core(near)

    def step_flows(now, pulled):
        new = jnp.maximum(now - STEP_PRIMAL * (flow_cost[0][:, None] - pulled), 0.0)
        return new, ((2.0 * new - now).astype(BF) * BF(-STEP_DUAL))

    ins = (duals2, stock2, stock_cost)
    packed = [jax.ShapeDtypeStruct((2 * size + tail, scenarios), BF)] * (parts - 1)
    packets = pl.pallas_call(
        functools.partial(pack_kernel, parts, size),
        out_shape=packed,
        in_specs=[pl.BlockSpec(memory_space=pltpu.HBM)] * len(ins),
        out_specs=[pl.BlockSpec(memory_space=pltpu.HBM)] * len(packed),
        scratch_shapes=[
            pltpu.VMEM(((parts - 1) * size, scenarios), F32),
            pltpu.VMEM(((parts - 1) * size, scenarios), F32),
            pltpu.VMEM(stock_cost.shape, F32),
        ]
        + [pltpu.VMEM(v.shape, v.dtype) for v in packed]
        + [
            pltpu.SemaphoreType.DMA((2 * (parts - 1),)),
            pltpu.SemaphoreType.DMA(()),
            pltpu.SemaphoreType.DMA((parts - 1,)),
        ],
        compiler_params=pltpu.CompilerParams(vmem_limit_bytes=FULL),
        cost_estimate=pl.CostEstimate(
            flops=0, bytes_accessed=12 * rows * scenarios, transcendentals=0
        ),
    )(*ins)
    packets = [rotate(packets[r - 1], "section", r) for r in range(1, parts)]

    stocks, *combined = call(
        functools.partial(first_stock_kernel, parts, size, tile),
        [jax.ShapeDtypeStruct((parts, size, scenarios), F32)] + [quarter] * parts,
        [],
        0,
        10 * rows * scenarios,
        duals2,
        stock2,
        stock_cost,
        *packets,
    )

    def first_pull(value):
        keep, send, slots_of = pl.pallas_call(
            functools.partial(first_pull_kernel, shape),
            out_shape=[half_blocks, half_blocks, jax.ShapeDtypeStruct((4, slots), jnp.int32)],
            in_specs=[SMEM] * 4 + [VMEM] * 2,
            out_specs=[VMEM, VMEM, SMEM],
            scratch_shapes=pull_scratch,
            compiler_params=pltpu.CompilerParams(vmem_limit_bytes=LIMIT),
        )(tile_row, tile_col, tile_live, block_place, tiles, value)
        return keep, swap_core(send), slots_of

    keep, send, slots_of = apart(first_pull, duals3)
    pulled = collect(keep, send, combined)
    flows1, bar1 = step_flows(flows2, pulled)
    combined = [combined[0]] + [rotate(combined[r], "section", -r) for r in range(1, parts)]
    near, far = spread(bar1, combined)

    duals1, half, *halves = call(
        functools.partial(push_step_kernel, parts, size),
        [jax.ShapeDtypeStruct((band_tiles, tile, scenarios), F32), whole_half]
        + [quarter3] * (parts - 1),
        push_scratch,
        flops,
        16 * rows * scenarios + 2 * slots * tile * tile,
        slots_of,
        tiles,
        duals3,
        demand3,
        near,
        far,
        *combined,
        smem=1,
    )
    halves = [rotate(halves[r - 1].reshape(size, scenarios), "section", r) for r in range(1, parts)]
    outs = call(
        functools.partial(last_stock_kernel, parts, size, tile),
        [jax.ShapeDtypeStruct((2 * size, scenarios), BF)] * parts,
        [],
        0,
        10 * rows * scenarios,
        duals1.reshape(rows, scenarios),
        stock_cost,
        *packets,
        stocks,
        *halves,
    )
    keep, send = call(
        pull_kernel,
        [half_blocks, half_blocks],
        pull_scratch[1:],
        flops,
        2 * rows * scenarios + 2 * slots * tile * tile,
        slots_of,
        tiles,
        half,
        smem=1,
    )
    send = swap_core(send)
    pulled = collect(keep, send, outs)
    outs = [outs[0]] + [rotate(outs[r], "section", -r) for r in range(1, parts)]
    flows2_out, bar2 = step_flows(flows1, pulled)
    near, far = spread(bar2, outs)
    duals_out = call(
        functools.partial(last_push_kernel, parts, size),
        jax.ShapeDtypeStruct((band_tiles, tile, scenarios), F32),
        [*push_scratch, pltpu.SemaphoreType.DMA(())],
        flops,
        14 * rows * scenarios + 2 * slots * tile * tile,
        slots_of,
        tiles,
        duals1,
        demand3,
        near,
        far,
        *outs,
        smem=1,
        spec=pl.BlockSpec(memory_space=pltpu.HBM),
    )
    stock_out = call(
        functools.partial(place_kernel, parts, size),
        jax.ShapeDtypeStruct((rows, scenarios), F32),
        [],
        0,
        6 * rows * scenarios,
        *outs,
    )
    return (
        flows2_out.reshape(flows.shape),
        stock_out.reshape(stock.shape),
        duals_out.reshape(duals.shape),
    )


def solution(mesh):
    in_specs = (
        P("section", "zone", None, None),
        P("section", "zone"),
        P("section", "zone"),
        P("section", "zone"),
        P(),
        P("section", "zone", None),
        P("section", "zone"),
        P("section", "zone"),
        P("section", "zone", None),
        P("section", "zone", None),
        P("section", "zone", None),
    )
    out_specs = (P("section", "zone", None), P("section", "zone", None), P("section", "zone", None))
    return jax.shard_map(
        per_device, mesh=mesh, in_specs=in_specs, out_specs=out_specs, check_vma=False
    )
```

```python
import functools

import jax
import jax.numpy as jnp
from jax import lax
from jax.experimental import pallas as pl
from jax.experimental.pallas import tpu as pltpu
from jax.sharding import PartitionSpec as P

ITERS = 2

STEP_PRIMAL = 0.25
STEP_DUAL = 0.25

BF = jnp.bfloat16
F32 = jnp.float32
VMEM = pl.BlockSpec(memory_space=pltpu.VMEM)
SMEM = pl.BlockSpec(memory_space=pltpu.SMEM)
LIMIT = 48 * 1024 * 1024
FULL = 62 * 1024 * 1024
CORES = 2
STEP_COST = 0


def rotate(value, axis, by):
    size = lax.axis_size(axis)
    return lax.ppermute(value, axis, [(i, (i + by) % size) for i in range(size)])


def rotate_chip(value, by):
    size = lax.axis_size("zone")
    return lax.ppermute(value, "zone", [(i, (i + by * CORES) % size) for i in range(size)])


def flip_chip(value, by):
    size = lax.axis_size("zone")
    return lax.ppermute(value, "zone", [(i, i ^ (by * CORES)) for i in range(size)])


def swap_core(value):
    size = lax.axis_size("zone")
    return lax.ppermute(value, "zone", [(i, i ^ 1) for i in range(size)])


def after(values, others):
    return lax.optimization_barrier((*values, *others))[: len(values)]


def call(kernel, outs, scratch, flops, moved, *args, smem=0, spec=VMEM):
    return pl.pallas_call(
        kernel,
        out_shape=outs,
        in_specs=[SMEM] * smem + [VMEM] * (len(args) - smem),
        out_specs=jax.tree.map(lambda _: spec, outs),
        scratch_shapes=scratch,
        compiler_params=pltpu.CompilerParams(vmem_limit_bytes=LIMIT),
        cost_estimate=pl.CostEstimate(flops=flops, bytes_accessed=moved, transcendentals=0),
    )(*args)


def quarter_rows(by, parts, size):
    part = lax.rem(lax.axis_index("section") + by, parts)
    return pl.ds(pl.multiple_of(part * size, size), size)


def pack_kernel(parts, size, *refs):
    duals_in, stock_in, cost_in = refs[:3]
    outs = refs[3 : 2 + parts]
    duals, stock, cost = refs[2 + parts : 5 + parts]
    packets = refs[5 + parts : 4 + 2 * parts]
    sems, cost_sem, out_sems = refs[4 + 2 * parts :]
    tile = packets[0].shape[1]
    pieces = size // tile
    cost_copy = pltpu.make_async_copy(cost_in, cost, cost_sem)
    cost_copy.start()
    gets, gives = [], []
    for r in range(1, parts):
        rows = quarter_rows(r, parts, size)
        here = pl.ds((r - 1) * size, size)
        for i, (there, held) in enumerate(((duals_in, duals), (stock_in, stock))):
            gets.append(
                pltpu.make_async_copy(there.at[rows], held.at[here], sems.at[2 * (r - 1) + i])
            )
            gets[-1].start()
        gives.append(pltpu.make_async_copy(packets[r - 1], outs[r - 1], out_sems.at[r - 1]))
    cost_copy.wait()
    for r in range(1, parts):
        part = lax.rem(lax.axis_index("section") + r, parts)
        packet = packets[r - 1]
        here = slice((r - 1) * size, r * size)
        tail = packet.shape[0] - 2 * size
        lines = [
            cost[:, pl.ds(pl.multiple_of(part * size + i * tile, tile), tile)]
            for i in range(pieces)
        ]
        lines.append(jnp.zeros((tail - pieces, tile), F32))
        packet[2 * size :] = jnp.concatenate(lines, axis=0).astype(BF)
        gets[2 * r - 2].wait()
        packet[0:size] = duals[here].astype(BF)
        gets[2 * r - 1].wait()
        packet[size : 2 * size] = stock[here].astype(BF)
        gives[r - 1].start()
    for give in gives:
        give.wait()


def block_slot(place, col, k, shape):
    chips, owned = shape
    zone = lax.axis_index("zone")
    chip, core = lax.div(zone, CORES), lax.rem(zone, CORES)
    position = place[col[0, k]]
    owner, inner = lax.div(position, owned), lax.rem(position, owned)
    differ = lax.div(owner, CORES) ^ chip
    away, step, bit = 0, chips // 2, 1
    while step:
        away = away + bit * lax.rem(lax.div(differ, step), 2)
        step, bit = step // 2, bit * 2
    half = jnp.where(lax.rem(owner, CORES) == core, 0, chips * owned)
    return half + away * owned + inner


def list_slots(shape, rows, row, col, live, place, slots):
    def step(k, carry):
        block = block_slot(place, col, k, shape)
        alive = live[0, k] == 1
        slots[0, k] = block
        slots[1, k] = jnp.where(alive, block, CORES * shape[0] * shape[1])
        slots[2, k] = row[0, k]
        slots[3, k] = jnp.where(alive, row[0, k], rows)
        return carry

    lax.fori_loop(0, slots.shape[1], step, 0)


def pull_slots(slots, tiles, half, acc):
    acc[...] = jnp.zeros_like(acc)

    def step(k, carry):
        acc[slots[1, k]] += lax.dot_general(
            tiles[k], half[slots[2, k]], (((0,), (0,)), ((), ())), preferred_element_type=F32
        )
        return carry

    lax.fori_loop(0, tiles.shape[0], step, 0, unroll=min(32, tiles.shape[0]))


def push_slots(slots, tiles, blocks, acc):
    def step(k, carry):
        acc[slots[3, k]] += jnp.dot(
            tiles[k], blocks[slots[0, k]], preferred_element_type=F32
        )
        return carry

    lax.fori_loop(0, tiles.shape[0], step, 0, unroll=min(32, tiles.shape[0]))


def give_partials(acc, keep, send):
    n = keep.shape[0]
    keep[...] = acc[0:n].astype(BF)
    send[...] = acc[n : 2 * n].astype(BF)


def first_pull_kernel(shape, row, col, live, place, tiles, duals, keep, send, slots, half, acc):
    list_slots(shape, duals.shape[0], row, col, live, place, slots)
    half[...] = duals[...].astype(BF)
    pull_slots(slots, tiles, half, acc)
    give_partials(acc, keep, send)


def pull_kernel(slots, tiles, half, keep, send, acc):
    pull_slots(slots, tiles, half, acc)
    give_partials(acc, keep, send)


def step_duals(parts, size, refs, blocks, acc):
    slots, tiles, duals, demand, near, far = refs[:6]
    combined = refs[6:]
    n = near.shape[0]
    blocks[0:n] = near[...]
    blocks[n : 2 * n] = far[...]
    pieces = size // tiles.shape[1]
    for r in range(parts):
        part = lax.rem(lax.axis_index("section") + r, parts)
        rows = pl.ds(part * pieces, pieces)
        acc[rows] = (
            duals[rows]
            + (STEP_DUAL * 0.25) * demand[rows].astype(F32)
            - STEP_DUAL * combined[r][0:size].astype(F32).reshape(pieces, *duals.shape[1:])
        )
    push_slots(slots, tiles, blocks, acc)


def push_step_kernel(parts, size, *refs):
    ins, next_duals, half = refs[: 6 + parts], refs[6 + parts], refs[7 + parts]
    packets, blocks, acc = refs[8 + parts : -2], refs[-2], refs[-1]
    tile = ins[1].shape[1]
    step_duals(parts, size, ins, blocks, acc)
    n = next_duals.shape[0]
    next_duals[...] = acc[0:n]
    half[...] = acc[0:n].astype(BF)
    pieces = size // tile
    for r in range(1, parts):
        part = lax.rem(lax.axis_index("section") + r, parts)
        packets[r - 1][...] = half[pl.ds(part * pieces, pieces)]


def place_kernel(parts, size, *refs):
    out = refs[parts]
    for r in range(parts):
        out[quarter_rows(r, parts, size), :] = refs[r][size:].astype(F32)


def push_kernel(slots, tiles, duals, demand, *refs):
    parts_of, (base, blocks, acc) = refs[:-3], refs[-3:]
    first = 0
    for part in parts_of:
        blocks[first : first + part.shape[0]] = part[...]
        first += part.shape[0]
    n = base.shape[0]
    acc[0:n] = duals[...] + (STEP_DUAL * 0.25) * demand[...].astype(F32)
    push_slots(slots, tiles, blocks, acc)
    base[...] = acc[0:n]


def final_kernel(parts, size, *refs):
    base, outs, (duals_out, stock_out) = refs[0], refs[1 : 1 + parts], refs[1 + parts : 3 + parts]
    duals, stock, sems = refs[3 + parts :]
    copies = []
    for r in range(parts):
        rows = quarter_rows(r, parts, size)
        duals[rows, :] = base[rows, :] - STEP_DUAL * outs[r][0:size].astype(F32)
        stock[rows, :] = outs[r][size:].astype(F32)
        for i, (held, out) in enumerate(((duals, duals_out), (stock, stock_out))):
            copies.append(pltpu.make_async_copy(held.at[rows], out.at[rows], sems.at[2 * r + i]))
            copies[-1].start()
    for copy in copies:
        copy.wait()


def own_rows(size, tile, i):
    return pl.ds(pl.multiple_of(lax.axis_index("section") * size + i * tile, tile), tile)


def eye_of(tile):
    return lax.broadcasted_iota(jnp.int32, (tile, tile), 0) == lax.broadcasted_iota(
        jnp.int32, (tile, tile), 1
    )


def stock_step(parts, lines, dual, stock, eye, ones):
    new = []
    for r in range(parts):
        line = jnp.where(eye, lines[r], 0.0).astype(BF)
        cost = jnp.dot(line, ones, preferred_element_type=F32)
        change = cost - dual[(r - 1) % parts] + dual[r]
        new.append(jnp.maximum(stock[r] - STEP_PRIMAL * change, 0.0))
    return new


def first_stock_kernel(parts, size, tile, *refs):
    own_duals, own_stock, own_cost, packets = *refs[:3], refs[3 : 2 + parts]
    stocks, combined = refs[2 + parts], refs[3 + parts :]
    eye, ones = eye_of(tile), jnp.ones((tile, tile), BF)
    costs = [None] + [packet[2 * size :].astype(F32) for packet in packets]
    for i in range(size // tile):
        rows = slice(i * tile, (i + 1) * tile)
        behind = slice(size + i * tile, size + (i + 1) * tile)
        own = own_rows(size, tile, i)
        dual = [own_duals[own, :]] + [packet[rows].astype(F32) for packet in packets]
        stock = [own_stock[own, :]] + [packet[behind].astype(F32) for packet in packets]
        lines = [own_cost[:, own]] + [c[i : i + 1] for c in costs[1:]]
        new = stock_step(parts, lines, dual, stock, eye, ones)
        bar = [2.0 * new[r] - stock[r] for r in range(parts)]
        for r in range(parts):
            stocks[r, rows] = new[r]
            combined[r][rows] = (bar[(r + 1) % parts] - bar[r]).astype(BF)


def last_stock_kernel(parts, size, tile, *refs):
    own_duals, own_cost, packets = *refs[:2], refs[2 : 1 + parts]
    stocks, duals, outs = refs[1 + parts], refs[2 + parts : 1 + 2 * parts], refs[1 + 2 * parts :]
    eye, ones = eye_of(tile), jnp.ones((tile, tile), BF)
    costs = [None] + [packet[2 * size :].astype(F32) for packet in packets]
    for i in range(size // tile):
        rows = slice(i * tile, (i + 1) * tile)
        behind = slice(size + i * tile, size + (i + 1) * tile)
        own = own_rows(size, tile, i)
        dual = [own_duals[own, :]] + [d[rows].astype(F32) for d in duals]
        stock = [stocks[r, rows] for r in range(parts)]
        lines = [own_cost[:, own]] + [c[i : i + 1] for c in costs[1:]]
        new = stock_step(parts, lines, dual, stock, eye, ones)
        bar = [2.0 * new[r] - stock[r] for r in range(parts)]
        for r in range(parts):
            outs[r][rows] = (bar[(r + 1) % parts] - bar[r]).astype(BF)
            outs[r][behind] = new[r].astype(BF)


def per_device(
    tiles,
    tile_row,
    tile_col,
    tile_live,
    block_place,
    demand,
    flow_cost,
    stock_cost,
    flows,
    stock,
    duals,
):
    unused_phases, slots, tile, unused_tile = tiles.shape
    scenarios = flows.shape[2]
    rows = duals.shape[1]
    parts = lax.axis_size("section")
    zones = lax.axis_size("zone")
    chips = zones // CORES
    blocks = block_place.shape[0]
    owned = blocks // zones
    band_tiles = rows // tile
    size = rows // parts
    shape = (chips, owned)
    tail = -(-(size // tile) // 16) * 16

    tiles = tiles.reshape(slots, tile, tile)
    duals2 = duals.reshape(rows, scenarios)
    stock2 = stock.reshape(rows, scenarios)
    flows2 = flows.reshape(owned * tile, scenarios)
    duals3 = duals.reshape(band_tiles, tile, scenarios)
    demand3 = demand.reshape(band_tiles, tile, scenarios)
    flops = 2 * slots * tile * tile * scenarios
    quarter = jax.ShapeDtypeStruct((size, scenarios), BF)
    quarter3 = jax.ShapeDtypeStruct((size // tile, tile, scenarios), BF)
    whole_half = jax.ShapeDtypeStruct((band_tiles, tile, scenarios), BF)
    half_blocks = jax.ShapeDtypeStruct((blocks // 2, tile, scenarios), BF)
    pull_scratch = [
        pltpu.VMEM((band_tiles, tile, scenarios), BF),
        pltpu.VMEM((blocks + 1, tile, scenarios), F32),
    ]
    push_scratch = [
        pltpu.VMEM((blocks, tile, scenarios), BF),
        pltpu.VMEM((band_tiles + 1, tile, scenarios), F32),
    ]

    known = block_place[0] >= 0

    def apart(f, *args):
        shapes = jax.eval_shape(f, *args)

        def none(*unused):
            return jax.tree.map(lambda v: jnp.zeros(v.shape, v.dtype), shapes)

        return lax.cond(known, f, none, *args)

    def add(value, other):
        return value.astype(F32) + other.astype(F32)

    def collect(keep, send, others):
        both = add(keep, send).astype(BF)
        parts_of = [both[k * owned : (k + 1) * owned] for k in range(chips)]
        got = []
        for k in range(1, chips):
            away = sum((chips // 2 >> i) * ((k >> i) & 1) for i in range(chips.bit_length()))
            got.append(flip_chip(parts_of[k], away))
        got = after(got, others)
        total = parts_of[0].astype(F32)
        for value in got:
            total = total + value.astype(F32)
        return total.reshape(owned * tile, scenarios)

    def spread(value, others, early=0, pieces=1):
        own = [value]
        step = chips // 2
        while step:
            if early and step == 1:
                first = flip_chip(value[:early], step)
                rest = flip_chip(jnp.concatenate([value[early:], *own[1:]], axis=0), step)
                own = own + [first, rest]
            else:
                own = own + [flip_chip(v, step) for v in own]
            step //= 2
        own = own[1:]
        own = after(own, others)
        near = jnp.concatenate([value, *own], axis=0).reshape(blocks // 2, tile, scenarios)
        piece = near.shape[0] // pieces
        return near, *(swap_core(near[i * piece : (i + 1) * piece]) for i in range(pieces))

    def step_flows(now, pulled):
        new = jnp.maximum(now - STEP_PRIMAL * (flow_cost[0][:, None] - pulled), 0.0)
        return new, ((2.0 * new - now).astype(BF) * BF(-STEP_DUAL))

    ins = (duals2, stock2, stock_cost)
    packed = [jax.ShapeDtypeStruct((2 * size + tail, scenarios), BF)] * (parts - 1)
    packets = pl.pallas_call(
        functools.partial(pack_kernel, parts, size),
        out_shape=packed,
        in_specs=[pl.BlockSpec(memory_space=pltpu.HBM)] * len(ins),
        out_specs=[pl.BlockSpec(memory_space=pltpu.HBM)] * len(packed),
        scratch_shapes=[
            pltpu.VMEM(((parts - 1) * size, scenarios), F32),
            pltpu.VMEM(((parts - 1) * size, scenarios), F32),
            pltpu.VMEM(stock_cost.shape, F32),
        ]
        + [pltpu.VMEM(v.shape, v.dtype) for v in packed]
        + [
            pltpu.SemaphoreType.DMA((2 * (parts - 1),)),
            pltpu.SemaphoreType.DMA(()),
            pltpu.SemaphoreType.DMA((parts - 1,)),
        ],
        compiler_params=pltpu.CompilerParams(vmem_limit_bytes=FULL),
        cost_estimate=pl.CostEstimate(
            flops=0, bytes_accessed=12 * rows * scenarios, transcendentals=0
        ),
    )(*ins)
    packets = [rotate(packets[r - 1], "section", r) for r in range(1, parts)]

    stocks, *combined = call(
        functools.partial(first_stock_kernel, parts, size, tile),
        [jax.ShapeDtypeStruct((parts, size, scenarios), F32)] + [quarter] * parts,
        [],
        0,
        10 * rows * scenarios,
        duals2,
        stock2,
        stock_cost,
        *packets,
    )

    def first_pull(value):
        keep, send, slots_of = pl.pallas_call(
            functools.partial(first_pull_kernel, shape),
            out_shape=[half_blocks, half_blocks, jax.ShapeDtypeStruct((4, slots), jnp.int32)],
            in_specs=[SMEM] * 4 + [VMEM] * 2,
            out_specs=[VMEM, VMEM, SMEM],
            scratch_shapes=pull_scratch,
            compiler_params=pltpu.CompilerParams(vmem_limit_bytes=LIMIT),
        )(tile_row, tile_col, tile_live, block_place, tiles, value)
        return keep, swap_core(send), slots_of

    keep, send, slots_of = apart(first_pull, duals3)
    pulled = collect(keep, send, combined)
    flows1, bar1 = step_flows(flows2, pulled)
    combined = [combined[0]] + [rotate(combined[r], "section", -r) for r in range(1, parts)]
    near, far = spread(bar1, combined, tile // 2)

    duals1, half, *halves = call(
        functools.partial(push_step_kernel, parts, size),
        [jax.ShapeDtypeStruct((band_tiles, tile, scenarios), F32), whole_half]
        + [quarter3] * (parts - 1),
        push_scratch,
        flops,
        16 * rows * scenarios + 2 * slots * tile * tile,
        slots_of,
        tiles,
        duals3,
        demand3,
        near,
        far,
        *combined,
        smem=1,
    )
    halves = [rotate(halves[r - 1].reshape(size, scenarios), "section", r) for r in range(1, parts)]
    outs = call(
        functools.partial(last_stock_kernel, parts, size, tile),
        [jax.ShapeDtypeStruct((2 * size, scenarios), BF)] * parts,
        [],
        0,
        10 * rows * scenarios,
        duals1.reshape(rows, scenarios),
        stock_cost,
        *packets,
        stocks,
        *halves,
    )
    keep, send = call(
        pull_kernel,
        [half_blocks, half_blocks],
        pull_scratch[1:],
        flops,
        2 * rows * scenarios + 2 * slots * tile * tile,
        slots_of,
        tiles,
        half,
        smem=1,
    )
    send = swap_core(send)
    pulled = collect(keep, send, outs)
    outs = [outs[0]] + [rotate(outs[r], "section", -r) for r in range(1, parts)]
    flows2_out, bar2 = step_flows(flows1, pulled)
    bar2, flows2_out = lax.optimization_barrier((bar2, flows2_out))
    near, *far = spread(bar2, [], pieces=4)
    base = call(
        push_kernel,
        jax.ShapeDtypeStruct((band_tiles, tile, scenarios), F32),
        push_scratch,
        0,
        0,
        slots_of,
        tiles,
        duals1,
        demand3,
        near,
        *far,
        smem=1,
    )
    whole = jax.ShapeDtypeStruct((rows, scenarios), F32)
    duals_out, stock_out = pl.pallas_call(
        functools.partial(final_kernel, parts, size),
        out_shape=[whole, whole],
        in_specs=[VMEM] * (parts + 1),
        out_specs=[pl.BlockSpec(memory_space=pltpu.HBM)] * 2,
        scratch_shapes=[pltpu.VMEM((rows, scenarios), F32)] * 2
        + [pltpu.SemaphoreType.DMA((2 * parts,))],
        compiler_params=pltpu.CompilerParams(vmem_limit_bytes=LIMIT),
        cost_estimate=pl.CostEstimate(
            flops=0, bytes_accessed=12 * rows * scenarios, transcendentals=0
        ),
    )(base.reshape(rows, scenarios), *outs)
    return (
        flows2_out.reshape(flows.shape),
        stock_out.reshape(stock.shape),
        duals_out.reshape(duals.shape),
    )


def solution(mesh):
    in_specs = (
        P("section", "zone", None, None),
        P("section", "zone"),
        P("section", "zone"),
        P("section", "zone"),
        P(),
        P("section", "zone", None),
        P("section", "zone"),
        P("section", "zone"),
        P("section", "zone", None),
        P("section", "zone", None),
        P("section", "zone", None),
    )
    out_specs = (P("section", "zone", None), P("section", "zone", None), P("section", "zone", None))
    return jax.shard_map(
        per_device, mesh=mesh, in_specs=in_specs, out_specs=out_specs, check_vma=False
    )
```

```python
import functools

import jax
import jax.numpy as jnp
from jax import lax
from jax.experimental import pallas as pl
from jax.experimental.pallas import tpu as pltpu
from jax.sharding import PartitionSpec as P

ITERS = 2

STEP_PRIMAL = 0.25
STEP_DUAL = 0.25

BF = jnp.bfloat16
F32 = jnp.float32
VMEM = pl.BlockSpec(memory_space=pltpu.VMEM)
SMEM = pl.BlockSpec(memory_space=pltpu.SMEM)
LIMIT = 48 * 1024 * 1024
FULL = 62 * 1024 * 1024
CORES = 2
STEP_COST = 0


def rotate(value, axis, by):
    size = lax.axis_size(axis)
    return lax.ppermute(value, axis, [(i, (i + by) % size) for i in range(size)])


def rotate_chip(value, by):
    size = lax.axis_size("zone")
    return lax.ppermute(value, "zone", [(i, (i + by * CORES) % size) for i in range(size)])


def flip_chip(value, by):
    size = lax.axis_size("zone")
    return lax.ppermute(value, "zone", [(i, i ^ (by * CORES)) for i in range(size)])


def swap_core(value):
    size = lax.axis_size("zone")
    return lax.ppermute(value, "zone", [(i, i ^ 1) for i in range(size)])


def after(values, others):
    return lax.optimization_barrier((*values, *others))[: len(values)]


def call(kernel, outs, scratch, flops, moved, *args, smem=0, spec=VMEM):
    return pl.pallas_call(
        kernel,
        out_shape=outs,
        in_specs=[SMEM] * smem + [VMEM] * (len(args) - smem),
        out_specs=jax.tree.map(lambda _: spec, outs),
        scratch_shapes=scratch,
        compiler_params=pltpu.CompilerParams(vmem_limit_bytes=LIMIT),
        cost_estimate=pl.CostEstimate(flops=flops, bytes_accessed=moved, transcendentals=0),
    )(*args)


def quarter_rows(by, parts, size):
    part = lax.rem(lax.axis_index("section") + by, parts)
    return pl.ds(pl.multiple_of(part * size, size), size)


def pack_kernel(parts, size, *refs):
    duals_in, stock_in, cost_in = refs[:3]
    outs = refs[3 : 2 + parts]
    duals, stock, cost = refs[2 + parts : 5 + parts]
    packets = refs[5 + parts : 4 + 2 * parts]
    sems, cost_sem, out_sems = refs[4 + 2 * parts :]
    tile = packets[0].shape[1]
    pieces = size // tile
    cost_copy = pltpu.make_async_copy(cost_in, cost, cost_sem)
    cost_copy.start()
    gets, gives = [], []
    for r in range(1, parts):
        rows = quarter_rows(r, parts, size)
        here = pl.ds((r - 1) * size, size)
        for i, (there, held) in enumerate(((duals_in, duals), (stock_in, stock))):
            gets.append(
                pltpu.make_async_copy(there.at[rows], held.at[here], sems.at[2 * (r - 1) + i])
            )
            gets[-1].start()
        gives.append(pltpu.make_async_copy(packets[r - 1], outs[r - 1], out_sems.at[r - 1]))
    cost_copy.wait()
    for r in range(1, parts):
        part = lax.rem(lax.axis_index("section") + r, parts)
        packet = packets[r - 1]
        here = slice((r - 1) * size, r * size)
        tail = packet.shape[0] - 2 * size
        lines = [
            cost[:, pl.ds(pl.multiple_of(part * size + i * tile, tile), tile)]
            for i in range(pieces)
        ]
        lines.append(jnp.zeros((tail - pieces, tile), F32))
        packet[2 * size :] = jnp.concatenate(lines, axis=0).astype(BF)
        gets[2 * r - 2].wait()
        packet[0:size] = duals[here].astype(BF)
        gets[2 * r - 1].wait()
        packet[size : 2 * size] = stock[here].astype(BF)
        gives[r - 1].start()
    for give in gives:
        give.wait()


def block_slot(place, col, k, shape):
    chips, owned = shape
    zone = lax.axis_index("zone")
    chip, core = lax.div(zone, CORES), lax.rem(zone, CORES)
    position = place[col[0, k]]
    owner, inner = lax.div(position, owned), lax.rem(position, owned)
    differ = lax.div(owner, CORES) ^ chip
    away, step, bit = 0, chips // 2, 1
    while step:
        away = away + bit * lax.rem(lax.div(differ, step), 2)
        step, bit = step // 2, bit * 2
    half = jnp.where(lax.rem(owner, CORES) == core, 0, chips * owned)
    return half + away * owned + inner


def list_slots(shape, rows, row, col, live, place, slots):
    def step(k, carry):
        block = block_slot(place, col, k, shape)
        alive = live[0, k] == 1
        slots[0, k] = block
        slots[1, k] = jnp.where(alive, block, CORES * shape[0] * shape[1])
        slots[2, k] = row[0, k]
        slots[3, k] = jnp.where(alive, row[0, k], rows)
        return carry

    lax.fori_loop(0, slots.shape[1], step, 0)


def pull_slots(slots, tiles, half, acc):
    acc[...] = jnp.zeros_like(acc)

    def step(k, carry):
        acc[slots[1, k]] += lax.dot_general(
            tiles[k], half[slots[2, k]], (((0,), (0,)), ((), ())), preferred_element_type=F32
        )
        return carry

    lax.fori_loop(0, tiles.shape[0], step, 0, unroll=min(32, tiles.shape[0]))


def push_slots(slots, tiles, blocks, acc):
    def step(k, carry):
        acc[slots[3, k]] += jnp.dot(
            tiles[k], blocks[slots[0, k]], preferred_element_type=F32
        )
        return carry

    lax.fori_loop(0, tiles.shape[0], step, 0, unroll=min(32, tiles.shape[0]))


def give_partials(acc, keep, send):
    n = keep.shape[0]
    keep[...] = acc[0:n].astype(BF)
    send[...] = acc[n : 2 * n].astype(BF)


def first_pull_kernel(shape, row, col, live, place, tiles, duals, keep, send, slots, half, acc):
    list_slots(shape, duals.shape[0], row, col, live, place, slots)
    half[...] = duals[...].astype(BF)
    pull_slots(slots, tiles, half, acc)
    give_partials(acc, keep, send)


def step_duals(parts, size, refs, blocks, acc):
    slots, tiles, duals, demand, near, far = refs[:6]
    combined = refs[6:]
    n = near.shape[0]
    blocks[0:n] = near[...]
    blocks[n : 2 * n] = far[...]
    pieces = size // tiles.shape[1]
    for r in range(parts):
        part = lax.rem(lax.axis_index("section") + r, parts)
        rows = pl.ds(part * pieces, pieces)
        acc[rows] = (
            duals[rows]
            + (STEP_DUAL * 0.25) * demand[rows].astype(F32)
            - STEP_DUAL * combined[r][0:size].astype(F32).reshape(pieces, *duals.shape[1:])
        )
    push_slots(slots, tiles, blocks, acc)


def push_pull_kernel(parts, size, *refs):
    ins, (next_duals, keep, send) = refs[: 6 + parts], refs[6 + parts : 9 + parts]
    packets, (blocks, half, acc, partials) = refs[9 + parts : -4], refs[-4:]
    slots, tiles = ins[:2]
    step_duals(parts, size, ins, blocks, acc)
    n = next_duals.shape[0]
    next_duals[...] = acc[0:n]
    half[...] = acc[0:n].astype(BF)
    pieces = n // parts
    for r in range(1, parts):
        part = lax.rem(lax.axis_index("section") + r, parts)
        packets[r - 1][...] = half[pl.ds(part * pieces, pieces)]
    pull_slots(slots, tiles, half, partials)
    give_partials(partials, keep, send)


def push_kernel(slots, tiles, duals, demand, *refs):
    parts_of, (base, blocks, acc) = refs[:-3], refs[-3:]
    first = 0
    for part in parts_of:
        blocks[first : first + part.shape[0]] = part[...]
        first += part.shape[0]
    n = base.shape[0]
    acc[0:n] = duals[...] + (STEP_DUAL * 0.25) * demand[...].astype(F32)
    push_slots(slots, tiles, blocks, acc)
    base[...] = acc[0:n]


def final_kernel(parts, size, *refs):
    base, outs, (duals_out, stock_out) = refs[0], refs[1 : 1 + parts], refs[1 + parts : 3 + parts]
    duals, stock, sems = refs[3 + parts :]
    copies = []
    for r in range(parts):
        rows = quarter_rows(r, parts, size)
        duals[rows, :] = base[rows, :] - STEP_DUAL * outs[r][0:size].astype(F32)
        stock[rows, :] = outs[r][size:].astype(F32)
        for i, (held, out) in enumerate(((duals, duals_out), (stock, stock_out))):
            copies.append(pltpu.make_async_copy(held.at[rows], out.at[rows], sems.at[2 * r + i]))
            copies[-1].start()
    for copy in copies:
        copy.wait()


def own_rows(size, tile, i):
    return pl.ds(pl.multiple_of(lax.axis_index("section") * size + i * tile, tile), tile)


def eye_of(tile):
    return lax.broadcasted_iota(jnp.int32, (tile, tile), 0) == lax.broadcasted_iota(
        jnp.int32, (tile, tile), 1
    )


def stock_step(parts, lines, dual, stock, eye, ones):
    new = []
    for r in range(parts):
        line = jnp.where(eye, lines[r], 0.0).astype(BF)
        cost = jnp.dot(line, ones, preferred_element_type=F32)
        change = cost - dual[(r - 1) % parts] + dual[r]
        new.append(jnp.maximum(stock[r] - STEP_PRIMAL * change, 0.0))
    return new


def first_stock_kernel(parts, size, tile, *refs):
    own_duals, own_stock, own_cost, packets = *refs[:3], refs[3 : 2 + parts]
    stocks, combined = refs[2 + parts], refs[3 + parts :]
    eye, ones = eye_of(tile), jnp.ones((tile, tile), BF)
    costs = [None] + [packet[2 * size :].astype(F32) for packet in packets]
    for i in range(size // tile):
        rows = slice(i * tile, (i + 1) * tile)
        behind = slice(size + i * tile, size + (i + 1) * tile)
        own = own_rows(size, tile, i)
        dual = [own_duals[own, :]] + [packet[rows].astype(F32) for packet in packets]
        stock = [own_stock[own, :]] + [packet[behind].astype(F32) for packet in packets]
        lines = [own_cost[:, own]] + [c[i : i + 1] for c in costs[1:]]
        new = stock_step(parts, lines, dual, stock, eye, ones)
        bar = [2.0 * new[r] - stock[r] for r in range(parts)]
        for r in range(parts):
            stocks[r, rows] = new[r]
            combined[r][rows] = (bar[(r + 1) % parts] - bar[r]).astype(BF)


def last_stock_kernel(parts, size, tile, *refs):
    own_duals, own_cost, packets = *refs[:2], refs[2 : 1 + parts]
    stocks, duals, outs = refs[1 + parts], refs[2 + parts : 1 + 2 * parts], refs[1 + 2 * parts :]
    eye, ones = eye_of(tile), jnp.ones((tile, tile), BF)
    costs = [None] + [packet[2 * size :].astype(F32) for packet in packets]
    for i in range(size // tile):
        rows = slice(i * tile, (i + 1) * tile)
        behind = slice(size + i * tile, size + (i + 1) * tile)
        own = own_rows(size, tile, i)
        dual = [own_duals[own, :]] + [d[rows].astype(F32) for d in duals]
        stock = [stocks[r, rows] for r in range(parts)]
        lines = [own_cost[:, own]] + [c[i : i + 1] for c in costs[1:]]
        new = stock_step(parts, lines, dual, stock, eye, ones)
        bar = [2.0 * new[r] - stock[r] for r in range(parts)]
        for r in range(parts):
            outs[r][rows] = (bar[(r + 1) % parts] - bar[r]).astype(BF)
            outs[r][behind] = new[r].astype(BF)


def per_device(
    tiles,
    tile_row,
    tile_col,
    tile_live,
    block_place,
    demand,
    flow_cost,
    stock_cost,
    flows,
    stock,
    duals,
):
    unused_phases, slots, tile, unused_tile = tiles.shape
    scenarios = flows.shape[2]
    rows = duals.shape[1]
    parts = lax.axis_size("section")
    zones = lax.axis_size("zone")
    chips = zones // CORES
    blocks = block_place.shape[0]
    owned = blocks // zones
    band_tiles = rows // tile
    size = rows // parts
    shape = (chips, owned)
    tail = -(-(size // tile) // 16) * 16

    tiles = tiles.reshape(slots, tile, tile)
    duals2 = duals.reshape(rows, scenarios)
    stock2 = stock.reshape(rows, scenarios)
    flows2 = flows.reshape(owned * tile, scenarios)
    duals3 = duals.reshape(band_tiles, tile, scenarios)
    demand3 = demand.reshape(band_tiles, tile, scenarios)
    flops = 2 * slots * tile * tile * scenarios
    quarter = jax.ShapeDtypeStruct((size, scenarios), BF)
    quarter3 = jax.ShapeDtypeStruct((size // tile, tile, scenarios), BF)
    half_blocks = jax.ShapeDtypeStruct((blocks // 2, tile, scenarios), BF)
    pull_scratch = [
        pltpu.VMEM((band_tiles, tile, scenarios), BF),
        pltpu.VMEM((blocks + 1, tile, scenarios), F32),
    ]
    push_scratch = [
        pltpu.VMEM((blocks, tile, scenarios), BF),
        pltpu.VMEM((band_tiles + 1, tile, scenarios), F32),
    ]

    known = block_place[0] >= 0

    def apart(f, *args):
        shapes = jax.eval_shape(f, *args)

        def none(*unused):
            return jax.tree.map(lambda v: jnp.zeros(v.shape, v.dtype), shapes)

        return lax.cond(known, f, none, *args)

    def add(value, other):
        return value.astype(F32) + other.astype(F32)

    def collect(keep, send, others):
        both = add(keep, send).astype(BF)
        parts_of = [both[k * owned : (k + 1) * owned] for k in range(chips)]
        got = []
        for k in range(1, chips):
            away = sum((chips // 2 >> i) * ((k >> i) & 1) for i in range(chips.bit_length()))
            got.append(flip_chip(parts_of[k], away))
        got = after(got, others)
        total = parts_of[0].astype(F32)
        for value in got:
            total = total + value.astype(F32)
        return total.reshape(owned * tile, scenarios)

    def spread(value, others, early=0, pieces=1):
        own = [value]
        step = chips // 2
        while step:
            if early and step == 1:
                first = flip_chip(value[:early], step)
                rest = flip_chip(jnp.concatenate([value[early:], *own[1:]], axis=0), step)
                own = own + [first, rest]
            else:
                own = own + [flip_chip(v, step) for v in own]
            step //= 2
        own = own[1:]
        own = after(own, others)
        near = jnp.concatenate([value, *own], axis=0).reshape(blocks // 2, tile, scenarios)
        piece = near.shape[0] // pieces
        return near, *(swap_core(near[i * piece : (i + 1) * piece]) for i in range(pieces))

    def step_flows(now, pulled):
        new = jnp.maximum(now - STEP_PRIMAL * (flow_cost[0][:, None] - pulled), 0.0)
        return new, ((2.0 * new - now).astype(BF) * BF(-STEP_DUAL))

    ins = (duals2, stock2, stock_cost)
    packed = [jax.ShapeDtypeStruct((2 * size + tail, scenarios), BF)] * (parts - 1)
    packets = pl.pallas_call(
        functools.partial(pack_kernel, parts, size),
        out_shape=packed,
        in_specs=[pl.BlockSpec(memory_space=pltpu.HBM)] * len(ins),
        out_specs=[pl.BlockSpec(memory_space=pltpu.HBM)] * len(packed),
        scratch_shapes=[
            pltpu.VMEM(((parts - 1) * size, scenarios), F32),
            pltpu.VMEM(((parts - 1) * size, scenarios), F32),
            pltpu.VMEM(stock_cost.shape, F32),
        ]
        + [pltpu.VMEM(v.shape, v.dtype) for v in packed]
        + [
            pltpu.SemaphoreType.DMA((2 * (parts - 1),)),
            pltpu.SemaphoreType.DMA(()),
            pltpu.SemaphoreType.DMA((parts - 1,)),
        ],
        compiler_params=pltpu.CompilerParams(vmem_limit_bytes=FULL),
        cost_estimate=pl.CostEstimate(
            flops=0, bytes_accessed=12 * rows * scenarios, transcendentals=0
        ),
    )(*ins)
    packets = [rotate(packets[r - 1], "section", r) for r in range(1, parts)]

    stocks, *combined = call(
        functools.partial(first_stock_kernel, parts, size, tile),
        [jax.ShapeDtypeStruct((parts, size, scenarios), F32)] + [quarter] * parts,
        [],
        0,
        10 * rows * scenarios,
        duals2,
        stock2,
        stock_cost,
        *packets,
    )

    def first_pull(value):
        keep, send, slots_of = pl.pallas_call(
            functools.partial(first_pull_kernel, shape),
            out_shape=[half_blocks, half_blocks, jax.ShapeDtypeStruct((4, slots), jnp.int32)],
            in_specs=[SMEM] * 4 + [VMEM] * 2,
            out_specs=[VMEM, VMEM, SMEM],
            scratch_shapes=pull_scratch,
            compiler_params=pltpu.CompilerParams(vmem_limit_bytes=LIMIT),
        )(tile_row, tile_col, tile_live, block_place, tiles, value)
        return keep, swap_core(send), slots_of

    keep, send, slots_of = apart(first_pull, duals3)
    pulled = collect(keep, send, combined)
    flows1, bar1 = step_flows(flows2, pulled)
    combined = [combined[0]] + [rotate(combined[r], "section", -r) for r in range(1, parts)]
    near, far = spread(bar1, combined, tile // 2)

    duals1, keep, send, *halves = call(
        functools.partial(push_pull_kernel, parts, size),
        [jax.ShapeDtypeStruct((band_tiles, tile, scenarios), F32), half_blocks, half_blocks]
        + [quarter3] * (parts - 1),
        [push_scratch[0], pull_scratch[0], push_scratch[1], pull_scratch[1]],
        flops,
        16 * rows * scenarios + 2 * slots * tile * tile,
        slots_of,
        tiles,
        duals3,
        demand3,
        near,
        far,
        *combined,
        smem=1,
    )
    halves = [rotate(halves[r - 1].reshape(size, scenarios), "section", r) for r in range(1, parts)]
    outs = call(
        functools.partial(last_stock_kernel, parts, size, tile),
        [jax.ShapeDtypeStruct((2 * size, scenarios), BF)] * parts,
        [],
        0,
        10 * rows * scenarios,
        duals1.reshape(rows, scenarios),
        stock_cost,
        *packets,
        stocks,
        *halves,
    )
    send = swap_core(send)
    pulled = collect(keep, send, outs)
    outs = [outs[0]] + [rotate(outs[r], "section", -r) for r in range(1, parts)]
    flows2_out, bar2 = step_flows(flows1, pulled)
    bar2, flows2_out = lax.optimization_barrier((bar2, flows2_out))
    near, *far = spread(bar2, [], pieces=4)
    base = call(
        push_kernel,
        jax.ShapeDtypeStruct((band_tiles, tile, scenarios), F32),
        push_scratch,
        0,
        0,
        slots_of,
        tiles,
        duals1,
        demand3,
        near,
        *far,
        smem=1,
    )
    whole = jax.ShapeDtypeStruct((rows, scenarios), F32)
    duals_out, stock_out = pl.pallas_call(
        functools.partial(final_kernel, parts, size),
        out_shape=[whole, whole],
        in_specs=[VMEM] * (parts + 1),
        out_specs=[pl.BlockSpec(memory_space=pltpu.HBM)] * 2,
        scratch_shapes=[pltpu.VMEM((rows, scenarios), F32)] * 2
        + [pltpu.SemaphoreType.DMA((2 * parts,))],
        compiler_params=pltpu.CompilerParams(vmem_limit_bytes=LIMIT),
        cost_estimate=pl.CostEstimate(
            flops=0, bytes_accessed=12 * rows * scenarios, transcendentals=0
        ),
    )(base.reshape(rows, scenarios), *outs)
    return (
        flows2_out.reshape(flows.shape),
        stock_out.reshape(stock.shape),
        duals_out.reshape(duals.shape),
    )


def solution(mesh):
    in_specs = (
        P("section", "zone", None, None),
        P("section", "zone"),
        P("section", "zone"),
        P("section", "zone"),
        P(),
        P("section", "zone", None),
        P("section", "zone"),
        P("section", "zone"),
        P("section", "zone", None),
        P("section", "zone", None),
        P("section", "zone", None),
    )
    out_specs = (P("section", "zone", None), P("section", "zone", None), P("section", "zone", None))
    return jax.shard_map(
        per_device, mesh=mesh, in_specs=in_specs, out_specs=out_specs, check_vma=False
    )
```

```python
import functools

import jax
import jax.numpy as jnp
from jax import lax
from jax.experimental import pallas as pl
from jax.experimental.pallas import tpu as pltpu
from jax.sharding import PartitionSpec as P

ITERS = 2

STEP_PRIMAL = 0.25
STEP_DUAL = 0.25

BF = jnp.bfloat16
F32 = jnp.float32
VMEM = pl.BlockSpec(memory_space=pltpu.VMEM)
SMEM = pl.BlockSpec(memory_space=pltpu.SMEM)
LIMIT = 48 * 1024 * 1024
FULL = 62 * 1024 * 1024
CORES = 2
STEP_COST = 0


def rotate(value, axis, by):
    size = lax.axis_size(axis)
    return lax.ppermute(value, axis, [(i, (i + by) % size) for i in range(size)])


def rotate_chip(value, by):
    size = lax.axis_size("zone")
    return lax.ppermute(value, "zone", [(i, (i + by * CORES) % size) for i in range(size)])


def flip_chip(value, by):
    size = lax.axis_size("zone")
    return lax.ppermute(value, "zone", [(i, i ^ (by * CORES)) for i in range(size)])


def swap_core(value):
    size = lax.axis_size("zone")
    return lax.ppermute(value, "zone", [(i, i ^ 1) for i in range(size)])


def after(values, others):
    return lax.optimization_barrier((*values, *others))[: len(values)]


def call(kernel, outs, scratch, flops, moved, *args, smem=0, spec=VMEM):
    return pl.pallas_call(
        kernel,
        out_shape=outs,
        in_specs=[SMEM] * smem + [VMEM] * (len(args) - smem),
        out_specs=jax.tree.map(lambda _: spec, outs),
        scratch_shapes=scratch,
        compiler_params=pltpu.CompilerParams(vmem_limit_bytes=LIMIT),
        cost_estimate=pl.CostEstimate(flops=flops, bytes_accessed=moved, transcendentals=0),
    )(*args)


def quarter_rows(by, parts, size):
    part = lax.rem(lax.axis_index("section") + by, parts)
    return pl.ds(pl.multiple_of(part * size, size), size)


def pack_kernel(parts, size, *refs):
    duals_in, stock_in, cost_in = refs[:3]
    outs = refs[3 : 2 + parts]
    duals, stock, cost = refs[2 + parts : 5 + parts]
    packets = refs[5 + parts : 4 + 2 * parts]
    sems, cost_sem, out_sems = refs[4 + 2 * parts :]
    tile = packets[0].shape[1]
    pieces = size // tile
    cost_copy = pltpu.make_async_copy(cost_in, cost, cost_sem)
    cost_copy.start()
    gets, gives = [], []
    for r in range(1, parts):
        rows = quarter_rows(r, parts, size)
        here = pl.ds((r - 1) * size, size)
        for i, (there, held) in enumerate(((duals_in, duals), (stock_in, stock))):
            gets.append(
                pltpu.make_async_copy(there.at[rows], held.at[here], sems.at[2 * (r - 1) + i])
            )
            gets[-1].start()
        gives.append(pltpu.make_async_copy(packets[r - 1], outs[r - 1], out_sems.at[r - 1]))
    cost_copy.wait()
    for r in range(1, parts):
        part = lax.rem(lax.axis_index("section") + r, parts)
        packet = packets[r - 1]
        here = slice((r - 1) * size, r * size)
        tail = packet.shape[0] - 2 * size
        lines = [
            cost[:, pl.ds(pl.multiple_of(part * size + i * tile, tile), tile)]
            for i in range(pieces)
        ]
        lines.append(jnp.zeros((tail - pieces, tile), F32))
        packet[2 * size :] = jnp.concatenate(lines, axis=0).astype(BF)
        gets[2 * r - 2].wait()
        packet[0:size] = duals[here].astype(BF)
        gets[2 * r - 1].wait()
        packet[size : 2 * size] = stock[here].astype(BF)
        gives[r - 1].start()
    for give in gives:
        give.wait()


def block_slot(place, col, k, shape):
    chips, owned = shape
    zone = lax.axis_index("zone")
    chip, core = lax.div(zone, CORES), lax.rem(zone, CORES)
    position = place[col[0, k]]
    owner, inner = lax.div(position, owned), lax.rem(position, owned)
    differ = lax.div(owner, CORES) ^ chip
    away, step, bit = 0, chips // 2, 1
    while step:
        away = away + bit * lax.rem(lax.div(differ, step), 2)
        step, bit = step // 2, bit * 2
    half = jnp.where(lax.rem(owner, CORES) == core, 0, chips * owned)
    return half + away * owned + inner


def list_slots(shape, rows, row, col, live, place, slots):
    def step(k, carry):
        block = block_slot(place, col, k, shape)
        alive = live[0, k] == 1
        slots[0, k] = block
        slots[1, k] = jnp.where(alive, block, CORES * shape[0] * shape[1])
        slots[2, k] = row[0, k]
        slots[3, k] = jnp.where(alive, row[0, k], rows)
        return carry

    lax.fori_loop(0, slots.shape[1], step, 0)


def pull_slots(slots, tiles, half, acc):
    acc[...] = jnp.zeros_like(acc)

    def step(k, carry):
        acc[slots[1, k]] += lax.dot_general(
            tiles[k], half[slots[2, k]], (((0,), (0,)), ((), ())), preferred_element_type=F32
        )
        return carry

    lax.fori_loop(0, tiles.shape[0], step, 0, unroll=min(32, tiles.shape[0]))


def push_slots(slots, tiles, blocks, acc):
    def step(k, carry):
        acc[slots[3, k]] += jnp.dot(
            tiles[k], blocks[slots[0, k]], preferred_element_type=F32
        )
        return carry

    lax.fori_loop(0, tiles.shape[0], step, 0, unroll=min(32, tiles.shape[0]))


def give_partials(acc, keep, send):
    n = keep.shape[0]
    keep[...] = acc[0:n].astype(BF)
    send[...] = acc[n : 2 * n].astype(BF)


def first_pull_kernel(shape, row, col, live, place, tiles, duals, keep, send, slots, half, acc):
    list_slots(shape, duals.shape[0], row, col, live, place, slots)
    half[...] = duals[...].astype(BF)
    pull_slots(slots, tiles, half, acc)
    give_partials(acc, keep, send)


def step_duals(parts, size, refs, blocks, acc):
    slots, tiles, duals, demand, near, far = refs[:6]
    combined = refs[6:]
    n = near.shape[0]
    blocks[0:n] = near[...]
    blocks[n : 2 * n] = far[...]
    pieces = size // tiles.shape[1]
    for r in range(parts):
        part = lax.rem(lax.axis_index("section") + r, parts)
        rows = pl.ds(part * pieces, pieces)
        acc[rows] = (
            duals[rows]
            + (STEP_DUAL * 0.25) * demand[rows].astype(F32)
            - STEP_DUAL * combined[r][0:size].astype(F32).reshape(pieces, *duals.shape[1:])
        )
    push_slots(slots, tiles, blocks, acc)


def push_pull_kernel(parts, size, *refs):
    ins, (next_duals, keep, send) = refs[: 6 + parts], refs[6 + parts : 9 + parts]
    packets, (blocks, half, acc, partials) = refs[9 + parts : -4], refs[-4:]
    slots, tiles = ins[:2]
    step_duals(parts, size, ins, blocks, acc)
    n = next_duals.shape[0]
    next_duals[...] = acc[0:n]
    half[...] = acc[0:n].astype(BF)
    pieces = n // parts
    for r in range(1, parts):
        part = lax.rem(lax.axis_index("section") + r, parts)
        packets[r - 1][...] = half[pl.ds(part * pieces, pieces)]
    pull_slots(slots, tiles, half, partials)
    give_partials(partials, keep, send)


def push_kernel(slots, tiles, duals, demand, now, pulled, cost, *refs):
    parts_of, (base, flows_out, blocks) = refs[:-3], refs[-3:]
    tile = now.shape[1]
    eye = eye_of(tile)
    for i in range(now.shape[0] // tile):
        rows = slice(i * tile, (i + 1) * tile)
        prices = jnp.sum(jnp.where(eye, cost[:, rows], 0.0), axis=1, keepdims=True)
        flows_out[rows, :] = jnp.maximum(
            now[rows, :] - STEP_PRIMAL * (prices - pulled[rows, :]), 0.0
        )
    first = 0
    for part in parts_of:
        blocks[first : first + part.shape[0]] = part[...]
        first += part.shape[0]
    n = duals.shape[0]
    base[0:n] = duals[...] + (STEP_DUAL * 0.25) * demand[...].astype(F32)
    push_slots(slots, tiles, blocks, base)


def final_kernel(parts, size, *refs):
    base, outs, (duals_out, stock_out) = refs[0], refs[1 : 1 + parts], refs[1 + parts : 3 + parts]
    duals, stock, sems = refs[3 + parts :]
    copies = []
    for r in range(parts):
        rows = quarter_rows(r, parts, size)
        duals[rows, :] = base[rows, :] - STEP_DUAL * outs[r][0:size].astype(F32)
        stock[rows, :] = outs[r][size:].astype(F32)
        for i, (held, out) in enumerate(((duals, duals_out), (stock, stock_out))):
            copies.append(pltpu.make_async_copy(held.at[rows], out.at[rows], sems.at[2 * r + i]))
            copies[-1].start()
    for copy in copies:
        copy.wait()


def own_rows(size, tile, i):
    return pl.ds(pl.multiple_of(lax.axis_index("section") * size + i * tile, tile), tile)


def eye_of(tile):
    return lax.broadcasted_iota(jnp.int32, (tile, tile), 0) == lax.broadcasted_iota(
        jnp.int32, (tile, tile), 1
    )


def stock_step(parts, lines, dual, stock, eye, ones):
    new = []
    for r in range(parts):
        line = jnp.where(eye, lines[r], 0.0).astype(BF)
        cost = jnp.dot(line, ones, preferred_element_type=F32)
        change = cost - dual[(r - 1) % parts] + dual[r]
        new.append(jnp.maximum(stock[r] - STEP_PRIMAL * change, 0.0))
    return new


def first_stock_kernel(parts, size, tile, *refs):
    own_duals, own_stock, own_cost, packets = *refs[:3], refs[3 : 2 + parts]
    stocks, combined = refs[2 + parts], refs[3 + parts :]
    eye, ones = eye_of(tile), jnp.ones((tile, tile), BF)
    costs = [None] + [packet[2 * size :].astype(F32) for packet in packets]
    for i in range(size // tile):
        rows = slice(i * tile, (i + 1) * tile)
        behind = slice(size + i * tile, size + (i + 1) * tile)
        own = own_rows(size, tile, i)
        dual = [own_duals[own, :]] + [packet[rows].astype(F32) for packet in packets]
        stock = [own_stock[own, :]] + [packet[behind].astype(F32) for packet in packets]
        lines = [own_cost[:, own]] + [c[i : i + 1] for c in costs[1:]]
        new = stock_step(parts, lines, dual, stock, eye, ones)
        bar = [2.0 * new[r] - stock[r] for r in range(parts)]
        for r in range(parts):
            stocks[r, rows] = new[r]
            combined[r][rows] = (bar[(r + 1) % parts] - bar[r]).astype(BF)


def last_stock_kernel(parts, size, tile, *refs):
    own_duals, own_cost, packets = *refs[:2], refs[2 : 1 + parts]
    stocks, duals, outs = refs[1 + parts], refs[2 + parts : 1 + 2 * parts], refs[1 + 2 * parts :]
    eye, ones = eye_of(tile), jnp.ones((tile, tile), BF)
    costs = [None] + [packet[2 * size :].astype(F32) for packet in packets]
    for i in range(size // tile):
        rows = slice(i * tile, (i + 1) * tile)
        behind = slice(size + i * tile, size + (i + 1) * tile)
        own = own_rows(size, tile, i)
        dual = [own_duals[own, :]] + [d[rows].astype(F32) for d in duals]
        stock = [stocks[r, rows] for r in range(parts)]
        lines = [own_cost[:, own]] + [c[i : i + 1] for c in costs[1:]]
        new = stock_step(parts, lines, dual, stock, eye, ones)
        bar = [2.0 * new[r] - stock[r] for r in range(parts)]
        for r in range(parts):
            outs[r][rows] = (bar[(r + 1) % parts] - bar[r]).astype(BF)
            outs[r][behind] = new[r].astype(BF)


def per_device(
    tiles,
    tile_row,
    tile_col,
    tile_live,
    block_place,
    demand,
    flow_cost,
    stock_cost,
    flows,
    stock,
    duals,
):
    unused_phases, slots, tile, unused_tile = tiles.shape
    scenarios = flows.shape[2]
    rows = duals.shape[1]
    parts = lax.axis_size("section")
    zones = lax.axis_size("zone")
    chips = zones // CORES
    blocks = block_place.shape[0]
    owned = blocks // zones
    band_tiles = rows // tile
    size = rows // parts
    shape = (chips, owned)
    tail = -(-(size // tile) // 16) * 16

    tiles = tiles.reshape(slots, tile, tile)
    duals2 = duals.reshape(rows, scenarios)
    stock2 = stock.reshape(rows, scenarios)
    flows2 = flows.reshape(owned * tile, scenarios)
    duals3 = duals.reshape(band_tiles, tile, scenarios)
    demand3 = demand.reshape(band_tiles, tile, scenarios)
    flops = 2 * slots * tile * tile * scenarios
    quarter = jax.ShapeDtypeStruct((size, scenarios), BF)
    quarter3 = jax.ShapeDtypeStruct((size // tile, tile, scenarios), BF)
    half_blocks = jax.ShapeDtypeStruct((blocks // 2, tile, scenarios), BF)
    pull_scratch = [
        pltpu.VMEM((band_tiles, tile, scenarios), BF),
        pltpu.VMEM((blocks + 1, tile, scenarios), F32),
    ]
    push_scratch = [
        pltpu.VMEM((blocks, tile, scenarios), BF),
        pltpu.VMEM((band_tiles + 1, tile, scenarios), F32),
    ]

    known = block_place[0] >= 0

    def apart(f, *args):
        shapes = jax.eval_shape(f, *args)

        def none(*unused):
            return jax.tree.map(lambda v: jnp.zeros(v.shape, v.dtype), shapes)

        return lax.cond(known, f, none, *args)

    def add(value, other):
        return value.astype(F32) + other.astype(F32)

    def collect(keep, send, others):
        both = add(keep, send).astype(BF)
        parts_of = [both[k * owned : (k + 1) * owned] for k in range(chips)]
        got = []
        for k in range(1, chips):
            away = sum((chips // 2 >> i) * ((k >> i) & 1) for i in range(chips.bit_length()))
            got.append(flip_chip(parts_of[k], away))
        got = after(got, others)
        total = parts_of[0].astype(F32)
        for value in got:
            total = total + value.astype(F32)
        return total.reshape(owned * tile, scenarios)

    def spread(value, others, early=0, pieces=1):
        own = [value]
        step = chips // 2
        while step:
            if early and step == 1:
                first = flip_chip(value[:early], step)
                rest = flip_chip(jnp.concatenate([value[early:], *own[1:]], axis=0), step)
                own = own + [first, rest]
            else:
                own = own + [flip_chip(v, step) for v in own]
            step //= 2
        own = own[1:]
        own = after(own, others)
        near = jnp.concatenate([value, *own], axis=0).reshape(blocks // 2, tile, scenarios)
        piece = near.shape[0] // pieces
        return near, *(swap_core(near[i * piece : (i + 1) * piece]) for i in range(pieces))

    def step_flows(now, pulled):
        new = jnp.maximum(now - STEP_PRIMAL * (flow_cost[0][:, None] - pulled), 0.0)
        return new, ((2.0 * new - now).astype(BF) * BF(-STEP_DUAL))

    ins = (duals2, stock2, stock_cost)
    packed = [jax.ShapeDtypeStruct((2 * size + tail, scenarios), BF)] * (parts - 1)
    packets = pl.pallas_call(
        functools.partial(pack_kernel, parts, size),
        out_shape=packed,
        in_specs=[pl.BlockSpec(memory_space=pltpu.HBM)] * len(ins),
        out_specs=[pl.BlockSpec(memory_space=pltpu.HBM)] * len(packed),
        scratch_shapes=[
            pltpu.VMEM(((parts - 1) * size, scenarios), F32),
            pltpu.VMEM(((parts - 1) * size, scenarios), F32),
            pltpu.VMEM(stock_cost.shape, F32),
        ]
        + [pltpu.VMEM(v.shape, v.dtype) for v in packed]
        + [
            pltpu.SemaphoreType.DMA((2 * (parts - 1),)),
            pltpu.SemaphoreType.DMA(()),
            pltpu.SemaphoreType.DMA((parts - 1,)),
        ],
        compiler_params=pltpu.CompilerParams(vmem_limit_bytes=FULL),
        cost_estimate=pl.CostEstimate(
            flops=0, bytes_accessed=12 * rows * scenarios, transcendentals=0
        ),
    )(*ins)
    packets = [rotate(packets[r - 1], "section", r) for r in range(1, parts)]

    stocks, *combined = call(
        functools.partial(first_stock_kernel, parts, size, tile),
        [jax.ShapeDtypeStruct((parts, size, scenarios), F32)] + [quarter] * parts,
        [],
        0,
        10 * rows * scenarios,
        duals2,
        stock2,
        stock_cost,
        *packets,
    )

    def first_pull(value):
        keep, send, slots_of = pl.pallas_call(
            functools.partial(first_pull_kernel, shape),
            out_shape=[half_blocks, half_blocks, jax.ShapeDtypeStruct((4, slots), jnp.int32)],
            in_specs=[SMEM] * 4 + [VMEM] * 2,
            out_specs=[VMEM, VMEM, SMEM],
            scratch_shapes=pull_scratch,
            compiler_params=pltpu.CompilerParams(vmem_limit_bytes=LIMIT),
        )(tile_row, tile_col, tile_live, block_place, tiles, value)
        return keep, swap_core(send), slots_of

    keep, send, slots_of = apart(first_pull, duals3)
    pulled = collect(keep, send, combined)
    flows1, bar1 = step_flows(flows2, pulled)
    combined = [combined[0]] + [rotate(combined[r], "section", -r) for r in range(1, parts)]
    near, far = spread(bar1, combined, tile // 2)

    duals1, keep, send, *halves = call(
        functools.partial(push_pull_kernel, parts, size),
        [jax.ShapeDtypeStruct((band_tiles, tile, scenarios), F32), half_blocks, half_blocks]
        + [quarter3] * (parts - 1),
        [push_scratch[0], pull_scratch[0], push_scratch[1], pull_scratch[1]],
        flops,
        16 * rows * scenarios + 2 * slots * tile * tile,
        slots_of,
        tiles,
        duals3,
        demand3,
        near,
        far,
        *combined,
        smem=1,
    )
    halves = [rotate(halves[r - 1].reshape(size, scenarios), "section", r) for r in range(1, parts)]
    outs = call(
        functools.partial(last_stock_kernel, parts, size, tile),
        [jax.ShapeDtypeStruct((2 * size, scenarios), BF)] * parts,
        [],
        0,
        10 * rows * scenarios,
        duals1.reshape(rows, scenarios),
        stock_cost,
        *packets,
        stocks,
        *halves,
    )
    send = swap_core(send)
    pulled = collect(keep, send, outs)
    outs = [outs[0]] + [rotate(outs[r], "section", -r) for r in range(1, parts)]
    unused, bar2 = step_flows(flows1, pulled)
    near, *far = spread(bar2, [], pieces=4)
    base, flows2_out = call(
        push_kernel,
        [
            jax.ShapeDtypeStruct((band_tiles + 1, tile, scenarios), F32),
            jax.ShapeDtypeStruct(flows2.shape, F32),
        ],
        push_scratch[:1],
        0,
        0,
        slots_of,
        tiles,
        duals1,
        demand3,
        flows1,
        pulled,
        flow_cost,
        near,
        *far,
        smem=1,
    )
    whole = jax.ShapeDtypeStruct((rows, scenarios), F32)
    duals_out, stock_out = pl.pallas_call(
        functools.partial(final_kernel, parts, size),
        out_shape=[whole, whole],
        in_specs=[VMEM] * (parts + 1),
        out_specs=[pl.BlockSpec(memory_space=pltpu.HBM)] * 2,
        scratch_shapes=[pltpu.VMEM((rows, scenarios), F32)] * 2
        + [pltpu.SemaphoreType.DMA((2 * parts,))],
        compiler_params=pltpu.CompilerParams(vmem_limit_bytes=LIMIT),
        cost_estimate=pl.CostEstimate(
            flops=0, bytes_accessed=12 * rows * scenarios, transcendentals=0
        ),
    )(base.reshape(rows + tile, scenarios), *outs)
    return (
        flows2_out.reshape(flows.shape),
        stock_out.reshape(stock.shape),
        duals_out.reshape(duals.shape),
    )


def solution(mesh):
    in_specs = (
        P("section", "zone", None, None),
        P("section", "zone"),
        P("section", "zone"),
        P("section", "zone"),
        P(),
        P("section", "zone", None),
        P("section", "zone"),
        P("section", "zone"),
        P("section", "zone", None),
        P("section", "zone", None),
        P("section", "zone", None),
    )
    out_specs = (P("section", "zone", None), P("section", "zone", None), P("section", "zone", None))
    return jax.shard_map(
        per_device, mesh=mesh, in_specs=in_specs, out_specs=out_specs, check_vma=False
    )
```
